512 devices in a mesh: face: 64 (over y, x, z_hi, core), band: 8 (over z_lo).
Axes of the slice: x: 4, y: 4, z: 16 (z_hi: 2, z_lo: 8; z = z_hi * 8 + z_lo), core: 2. Of those that a mesh axis runs over, the one named last changes fastest.
Arguments:
- code_ids: int32 [8, 256, 1024], P('band', None, 'face'), may hold values from 0 to 63999, as said below
- projection: float32 [6, 96], replicated, may hold values from -2.5 to 2.5
- first_weight: bfloat16 [9, 96, 96], replicated, may hold values from -0.21875 to 0.21875
- second_weight: bfloat16 [9, 96, 96], replicated, may hold values from -0.21875 to 0.21875
- norm_gain: float32 [96], replicated, may hold values from 0.5 to 1.5
- norm_shift: float32 [96], replicated, may hold values from -3 to 3
- cotangent: bfloat16 [1024, 768, 256], P('face', 'band'), may hold values from -0.009765625 to 0.009765625
Outputs:
- mixed: bfloat16 [1024, 768, 256], P('face', 'band')
- first_grad: float32 [9, 96, 96], P(None, 'band')
- second_grad: float32 [9, 96, 96], P(None, 'band')
- gain_grad: float32 [96], replicated
- shift_grad: float32 [96], replicated
- projection_grad: float32 [6, 96], replicated
The draws below stay inside these ranges and needn't reach their ends.
Inputs may be any that keep to these rules, and one draw needn't show every extreme that they name: `code_ids`: six-digit mixed-radix codes, digits of 8, 8, 8, 5, 5, 5 levels, lowest digit first.
All inputs are finite; a program needn't handle non-finite values.
Results may differ from the reference program's by a relative error of at most 0.013.
Values may be sent and summed in bfloat16 or wider, within the bound.
A program may use at most 64 MiB of HBM per device.

```python
import jax
import jax.numpy as jnp
from jax import lax

FRAMES = 8
CHANNELS = 96
GROUPS = 32
ROWS = 256
STRIP = 1024


def draw_code_ids(key, part):
    key = jax.random.fold_in(key, 11)
    shape = (FRAMES, ROWS, STRIP)
    column = lax.broadcasted_iota(jnp.int32, shape, 2)
    row_index = lax.broadcasted_iota(jnp.int32, shape, 1)
    frame_index = lax.broadcasted_iota(jnp.int32, shape, 0)
    block_width = max(STRIP // 16, 1)
    block_count = -(-STRIP // block_width)
    packed = jnp.zeros(shape, jnp.int32)
    stride = 1
    for digit_index, level_count in enumerate((8, 8, 8, 5, 5, 5)):
        spread = 2 + (level_count - 2) * column // max(STRIP - 1, 1)
        centre = jax.random.randint(jax.random.fold_in(key, 100 + digit_index), (FRAMES, 1, 1), 0, level_count)
        block_jitter = jax.random.randint(jax.random.fold_in(key, 200 + digit_index), (block_count,), -1, 2)
        jitter = jnp.repeat(block_jitter, block_width)[:STRIP][None, None, :]
        lowest = jnp.clip(centre + jitter - spread // 2, 0, level_count - spread)
        random_bits = jax.random.randint(jax.random.fold_in(key, digit_index), shape, 0, 1 << 20)
        packed = packed + (lowest + random_bits % spread) * stride
        stride = stride * level_count
    corner = (frame_index == 0) & (column == STRIP - 1)
    packed = jnp.where(corner & (row_index == 0), 63999, packed)
    packed = jnp.where(corner & (row_index == ROWS - 1), 0, packed)
    return packed


def block_scale(rng, dims, pieces, least, top_value):
    def one(dim, parts):
        steps = jax.random.uniform(jax.random.fold_in(jax.random.fold_in(rng, 6), dim), (parts,), jnp.float32, least / len(pieces), top_value / len(pieces))
        return jnp.repeat(jnp.exp(steps), dims[dim] // parts).reshape((-1,) + (1,) * (len(dims) - dim - 1))

    gain = one(*pieces[0])
    for cut in pieces[1:]:
        gain = gain * one(*cut)
    return gain


def centred(key, extent, scale, most, shards=(), kind=jnp.bfloat16):
    array = jax.random.normal(key, extent, jnp.float32) * scale
    if len(shards) > 0:
        array = block_scale(key, extent, shards, -0.22, 0.18) * array
    return jnp.clip(array, min=-most, max=most).astype(kind)


def setup_inputs(seed: int = 0) -> dict:
    splits = jax.random.split(jax.random.key(seed), 8)
    code_ids = draw_code_ids(jax.random.fold_in(splits[7], 71), 0)
    projection = centred(splits[1], (6, CHANNELS), 6 ** -0.5, 2.5, (), jnp.float32)
    first_weight = centred(splits[2], (9, CHANNELS, CHANNELS), (9 * CHANNELS) ** -0.5, 0.21875)
    second_weight = centred(splits[3], (9, CHANNELS, CHANNELS), (9 * CHANNELS) ** -0.5, 0.21875)
    norm_gain = jnp.clip(jax.random.uniform(splits[4], (CHANNELS,), jnp.float32, 0.5, 1.5), 0.5, 1.5)
    norm_shift = centred(splits[5], (CHANNELS,), 0.5, 3.0, (), jnp.float32)
    cotangent = centred(splits[6], (STRIP, FRAMES * CHANNELS, ROWS), (1.0 / (FRAMES * ROWS * STRIP) ** 0.5), 0.009765625, ((0, 64), (1, 8)))
    return {"code_ids": code_ids, "projection": projection, "first_weight": first_weight, "second_weight": second_weight, "norm_gain": norm_gain, "norm_shift": norm_shift, "cotangent": cotangent}


code_levels = (8, 8, 8, 5, 5, 5)
code_strides = (1, 8, 64, 512, 2560, 12800)

def decode(code_ids):
    values = []
    for level_count, stride in zip(code_levels, code_strides):
        digits = code_ids // stride % level_count
        values.append((2.0 * digits.astype(jnp.float32) - (level_count - 1)) / level_count)
    return jnp.stack(values)

def shifted(field, down, right):
    height = field.shape[1]
    padded = jnp.pad(field, ((0, 0), (1, 1), (0, 0)))
    return jnp.roll(padded[:, 1 + down:1 + down + height, :], -right, axis=2)

def conv_ahead(field, weights):
    summed = None
    for tap_index in range(9):
        moved = shifted(field, tap_index // 3 - 1, tap_index % 3 - 1)
        contribution = jnp.einsum('ihw,io->ohw', moved, weights[tap_index])
        summed = contribution if summed is None else summed + contribution
    return summed

def conv_behind(grads, weights):
    summed = None
    for tap_index in range(9):
        moved = shifted(grads, 1 - tap_index // 3, 1 - tap_index % 3)
        contribution = jnp.einsum('ohw,io->ihw', moved, weights[tap_index])
        summed = contribution if summed is None else summed + contribution
    return summed

def weight_terms(field, grads):
    return jnp.stack([jnp.einsum('ihw,ohw->io', shifted(field, tap_index // 3 - 1, tap_index % 3 - 1), grads) for tap_index in range(9)])

def group_total(values):
    sums = values.reshape(GROUPS, -1).sum(axis=1)
    return jnp.repeat(sums, values.shape[0] // GROUPS)

def reference(code_ids, projection, first_weight, second_weight, norm_gain, norm_shift, cotangent):
    weights_one = first_weight.astype(jnp.float32)
    weights_two = second_weight.astype(jnp.float32)
    cot_field = jnp.transpose(cotangent.reshape(STRIP, FRAMES, CHANNELS, ROWS), (1, 2, 3, 0))

    def lift(frame_codes):
        latent = decode(frame_codes)
        lifted = jnp.einsum('khw,ko->ohw', latent, projection, precision=lax.Precision.HIGHEST).astype(jnp.bfloat16)
        return (latent, lifted)

    def first_pass(frame_codes):
        return conv_ahead(lift(frame_codes)[1].astype(jnp.float32), weights_one)
    first_out = lax.map(first_pass, code_ids)
    count = float(CHANNELS // GROUPS * FRAMES * ROWS * STRIP)
    channel_sums = lax.optimization_barrier(jnp.sum(lax.map(lambda frame_block: lax.optimization_barrier(jnp.sum(frame_block, axis=(1, 2))), first_out), axis=0))
    mean = group_total(channel_sums) / count
    squares = lax.optimization_barrier(jnp.sum(lax.map(lambda frame_block: lax.optimization_barrier(jnp.sum((frame_block - mean[:, None, None]) ** 2, axis=(1, 2))), first_out), axis=0))
    variance = group_total(squares) / count
    scale = 1.0 / jnp.sqrt(variance + 1e-05)
    gain_col = norm_gain[:, None, None]
    shift_col = norm_shift[:, None, None]
    mean_col = mean[:, None, None]
    scale_col = scale[:, None, None]

    def forward_step(carry, inputs):
        second_sum, shift_sum, gain_sum = carry
        frame_first, frame_cot, frame_codes = inputs
        lifted = lift(frame_codes)[1]
        standard = (frame_first - mean_col) * scale_col
        pre_act = standard * gain_col + shift_col
        activated = jax.nn.silu(pre_act).astype(jnp.bfloat16)
        act_float = activated.astype(jnp.float32)
        second_out = conv_ahead(act_float, weights_two)
        mixed = (lifted.astype(jnp.float32) + second_out).astype(jnp.bfloat16)
        cot_float = frame_cot.astype(jnp.float32)
        second_sum = second_sum + weight_terms(act_float, cot_float)
        act_grad = conv_behind(cot_float, weights_two)
        sigma = jax.nn.sigmoid(pre_act)
        pre_grad = act_grad * sigma * (1.0 + pre_act * (1.0 - sigma))
        shift_sum = shift_sum + lax.optimization_barrier(jnp.sum(pre_grad, axis=(1, 2)))
        gain_sum = gain_sum + lax.optimization_barrier(jnp.sum(pre_grad * standard, axis=(1, 2)))
        return ((second_sum, shift_sum, gain_sum), (mixed, pre_grad))
    start_one = (jnp.zeros((9, CHANNELS, CHANNELS), jnp.float32), jnp.zeros((CHANNELS,), jnp.float32), jnp.zeros((CHANNELS,), jnp.float32))
    (second_grad, shift_grad, gain_grad), (mixed_field, pre_grads) = lax.scan(forward_step, start_one, (first_out, cot_field, code_ids))
    first_mean = (group_total(norm_gain * shift_grad) / count)[:, None, None]
    second_mean = (group_total(norm_gain * gain_grad) / count)[:, None, None]

    def backward_step(carry, inputs):
        first_sum, proj_sum = carry
        frame_first, pre_grad, frame_cot, frame_codes = inputs
        latent, lifted = lift(frame_codes)
        standard = (frame_first - mean_col) * scale_col
        in_grad = (scale_col * (pre_grad * gain_col - first_mean - standard * second_mean)).astype(jnp.bfloat16)
        in_float = in_grad.astype(jnp.float32)
        first_sum = first_sum + weight_terms(lifted.astype(jnp.float32), in_float)
        lifted_grad = frame_cot.astype(jnp.float32) + conv_behind(in_float, weights_one)
        proj_sum = proj_sum + jnp.einsum('khw,ohw->ko', latent, lifted_grad, precision=lax.Precision.HIGHEST)
        return ((first_sum, proj_sum), None)
    start_two = (jnp.zeros((9, CHANNELS, CHANNELS), jnp.float32), jnp.zeros((6, CHANNELS), jnp.float32))
    (first_grad, projection_grad), unused = lax.scan(backward_step, start_two, (first_out, pre_grads, cot_field, code_ids))
    mixed = jnp.transpose(mixed_field, (3, 0, 1, 2)).reshape(STRIP, FRAMES * CHANNELS, ROWS)
    return (mixed, first_grad, second_grad, gain_grad, shift_grad, projection_grad)
```

```python
import jax
import jax.numpy as jnp
from jax import lax
from jax.experimental import pallas as pl
from jax.experimental.pallas import tpu as pltpu
from jax.sharding import PartitionSpec as P

MESH = pl.DeviceIdType.MESH
HIGHEST = lax.Precision.HIGHEST
F32, BF16 = jnp.float32, jnp.bfloat16

CH, ROWS, COLS = 96, 256, 16
PLANE, LINE, BANDS = 32, 16, 8
CHUNKS = 27
POSITIONS = float(2**21)
ONE = 46


def iota(shape, dim):
    return lax.broadcasted_iota(jnp.int32, shape, dim)


def dot(a, b):
    return lax.dot_general(a, b, (((1,), (0,)), ((), ())), preferred_element_type=F32)


def dot_t(a, b):
    return lax.dot_general(a, b, (((1,), (1,)), ((), ())), preferred_element_type=F32)


def dot32(a, b):
    return lax.dot_general(
        a, b, (((1,), (0,)), ((), ())), precision=HIGHEST, preferred_element_type=F32
    )


def dot32_t(a, b):
    return lax.dot_general(
        a, b, (((1,), (1,)), ((), ())), precision=HIGHEST, preferred_element_type=F32
    )


def pieces(value, count):
    parts = []
    for _ in range(count):
        part = value.astype(BF16).astype(F32)
        parts.append(part)
        value = value - part
    return parts


def later(value, lane):
    return jnp.where(lane == 0, 0.0, pltpu.roll(value, 1, 1))


def earlier(value, lane):
    return jnp.where(lane == ROWS - 1, 0.0, pltpu.roll(value, ROWS - 1, 1))


def unit_row(index):
    if index < 27:
        return index // 9 * 32 + index // 3 % 3 * 8 + index % 3 * 2
    return 96 + 2 * (index - 27) if index < 30 else ONE


def kernel(
    code_ref, proj_ref, w1_ref, w2_ref, gain_ref, shift_ref, cot_ref,
    mixed_ref, first_ref, second_ref, gain_out, shift_out, proj_out,
    own, edge_l, edge_r, halo_l, halo_r,
    digits, cots, acts, grads, w2p, w2t, back_w, ahead_w, p8, wt,
    gs, g_rs, g_z, g_ag, g_all,
    sg, sg_send, sg_recv, af, af_send, af_recv, z_send, z_recv, ag,
    halo_send_sem, halo_recv_sem, send_sem, recv_sem,
):
    face, band = lax.axis_index("face"), lax.axis_index("band")
    core, z_hi, yx = face % 2, face // 2 % 2, face // 4
    q, z = yx * 2 + core, z_hi * BANDS + band

    def plane(j):
        return (j // 2 * 4 + z_hi * 2 + j % 2, band)

    def line(j):
        return (yx * 4 + j // BANDS * 2 + core, j % BANDS)

    left, right = ((face + 63) % 64, band), ((face + 1) % 64, band)

    barrier = pltpu.get_barrier_semaphore()
    for target in (left, right):
        pl.semaphore_signal(barrier, 1, device_id=target, device_id_type=MESH)
    for j in range(PLANE):
        @pl.when(q != j)
        def _():
            pl.semaphore_signal(barrier, 1, device_id=plane(j), device_id_type=MESH)
    for j in range(LINE):
        @pl.when(z != j)
        def _():
            pl.semaphore_signal(barrier, 1, device_id=line(j), device_id_type=MESH)

    def send(src, dst, sem, target):
        return pltpu.make_async_remote_copy(
            src, dst, send_sem.at[sem], recv_sem.at[sem], device_id=target, device_id_type=MESH
        )

    lane = iota((8, ROWS), 1)
    wide = iota((CH, ROWS), 1)

    codes = jnp.transpose(code_ref[0].astype(F32))
    own[...] = codes
    edge_l[...] = codes[0:2]
    edge_r[...] = codes[COLS - 2 : COLS]

    place, channel = iota((CH, CH), 0), iota((CH, CH), 1)
    perm = (channel == place % 32 // 4 * 12 + place // 32 * 4 + place % 4).astype(BF16)
    eye = (channel == place).astype(BF16)
    same_group = (channel // 3 == place // 3).astype(F32)
    for dc in range(3):
        for dr in range(3):
            tap, at = dr * 3 + dc, dc * 3 + dr
            w2p[pl.ds(at * CH, CH), :] = dot(perm, w2_ref[tap]).astype(BF16)
            back = (2 - dc) * 3 + dr
            w2t[pl.ds(back * CH, CH), :] = dot_t(eye, w2p[pl.ds(at * CH, CH), :]).astype(BF16)
    ahead_w[...] = dot_t(eye, w2p[...]).astype(BF16)
    back_w[...] = dot_t(eye, w2t[...]).astype(BF16)

    pl.semaphore_wait(barrier, PLANE - 1 + LINE - 1 + 2)

    to_right = pltpu.make_async_remote_copy(
        edge_r, halo_l, halo_send_sem.at[0], halo_recv_sem.at[0], device_id=right, device_id_type=MESH
    )
    to_left = pltpu.make_async_remote_copy(
        edge_l, halo_r, halo_send_sem.at[1], halo_recv_sem.at[1], device_id=left, device_id_type=MESH
    )
    to_right.start()
    to_left.start()

    level = jnp.where(iota((8, 1), 0) < 3, 8.0, 5.0)
    p8[...] = jnp.zeros_like(p8)
    p8[0:6, 0:CH] = proj_ref[...] / level[0:6]
    proj8 = p8[:, 0:CH]
    proj_parts = pieces(proj8, 3)
    proj_rows = jnp.concatenate(proj_parts + [jnp.zeros_like(proj8)], axis=0).astype(BF16)
    for dc in range(3):
        for dr in range(3):
            got = dot(proj_rows, w1_ref[dr * 3 + dc])
            wt[pl.ds(dc * 32 + dr * 8, 8), :] = got[0:8] + got[8:16] + got[16:24]
        wt[pl.ds(dc * 32 + 24, 8), :] = jnp.zeros((8, CH), F32)
    no_rows = jnp.zeros_like(proj8)
    lift_w = jnp.concatenate(
        [
            dot_t(eye, jnp.concatenate([no_rows, part, no_rows, no_rows], axis=0).astype(BF16))
            for part in proj_parts
        ],
        axis=0,
    ).astype(BF16)

    cots[0:2] = jnp.zeros((2, 3, CH, ROWS), BF16)
    cots[COLS + 2 : COLS + 4] = jnp.zeros((2, 3, CH, ROWS), BF16)

    def cot_step(c, carry):
        value = cot_ref[c]
        wider = value.astype(F32)
        cots[c + 2, 0] = earlier(wider, wide).astype(BF16)
        cots[c + 2, 1] = value
        cots[c + 2, 2] = later(wider, wide).astype(BF16)
        return carry

    lax.fori_loop(0, COLS, cot_step, 0)

    to_right.wait()
    to_left.wait()

    index = iota((8, 1), 0)
    stride = jnp.where(
        index == 0, 1.0, jnp.where(index == 1, 8.0, jnp.where(index == 2, 64.0,
        jnp.where(index == 3, 512.0, jnp.where(index == 4, 2560.0, 12800.0)))))
    per_stride, per_level = 1.0 / stride, 1.0 / level
    for c in range(COLS + 4):
        if c < 2:
            row = halo_l[c : c + 1, :]
        elif c < COLS + 2:
            row = own[c - 2 : c - 1, :]
        else:
            row = halo_r[c - COLS - 2 : c - COLS - 1, :]
        quotient = jnp.floor((row + 0.5) * per_stride)
        digit = quotient - level * jnp.floor((quotient + 0.5) * per_level)
        value = jnp.where(index < 6, 2.0 * digit - (level - 1.0), 0.0)
        block = [later(value, lane), jnp.where(index == 6, 1.0, value), earlier(value, lane)]
        digits[c] = jnp.concatenate(block + [jnp.zeros_like(value)], axis=0).astype(BF16)
    digits[COLS + 4 : COLS + 8] = jnp.zeros((4, 32, ROWS), BF16)

    gram = None
    for c in range(COLS):
        term = dot_t(digits[c + 2], digits[c + 2 : c + 6].reshape(128, ROWS))
        gram = term if gram is None else gram + term
    for j in range(PLANE):
        gs[j] = gram[j : j + 1]
    for j in range(PLANE):
        @pl.when(q != j)
        def _():
            send(gs.at[j], g_rs.at[q], 0, plane(j)).start()
    g_rs[q] = gs[q]

    def grad_step(c, carry):
        grads[c] = dot(back_w[...], cots[pl.ds(c, 3)].reshape(9 * CH, ROWS))
        return carry

    lax.fori_loop(0, 6, grad_step, 0)
    some = send(gs.at[pl.ds(0, PLANE - 1)], g_rs.at[pl.ds(0, PLANE - 1)], 0, right)
    some.wait()
    g_z[z] = jnp.sum(g_rs[...], axis=0)
    for j in range(LINE):
        @pl.when(z != j)
        def _():
            send(g_z.at[z], g_z.at[z], 1, line(j)).start()
    lax.fori_loop(6, 12, grad_step, 0)
    send(g_z.at[pl.ds(0, LINE - 1)], g_z.at[pl.ds(0, LINE - 1)], 1, right).wait()
    g_ag[q] = jnp.sum(g_z[...], axis=0)
    for j in range(PLANE):
        @pl.when(q != j)
        def _():
            send(g_ag.at[q], g_ag.at[q], 2, plane(j)).start()
    lax.fori_loop(12, 18, grad_step, 0)
    send(g_ag.at[pl.ds(0, PLANE - 1)], g_ag.at[pl.ds(0, PLANE - 1)], 2, right).wait()
    for j in range(PLANE):
        g_all[j : j + 1, :] = g_ag[j]
    g_all[PLANE:128, :] = jnp.zeros((128 - PLANE, 128), F32)

    near = g_all[0:32, :]
    flipped = jnp.transpose(g_all[...])
    lane32 = iota((32, 128), 1)
    gram_all = jnp.concatenate(
        [
            near,
            jnp.where(lane32 < 32, flipped[32:64], pltpu.roll(near, 32, 1)),
            jnp.where(
                lane32 < 32,
                flipped[64:96],
                jnp.where(lane32 < 64, pltpu.roll(flipped[32:64], 32, 1), pltpu.roll(near, 64, 1)),
            ),
        ],
        axis=0,
    )[:, 0:CH]
    digit_sum = gram_all[:, ONE : ONE + 1]
    digit_mean = digit_sum / POSITIONS
    covariance = gram_all / POSITIONS - digit_mean * (gram_all[ONE : ONE + 1, :] / POSITIONS)
    weights = wt[...]
    spread = dot32(covariance, weights)

    def by_group(value):
        return dot32(jnp.broadcast_to(value, (8, CH)), same_group)[0:1]

    channel_mean = jnp.sum(weights * digit_mean, axis=0, keepdims=True)
    mean = by_group(channel_mean) / 3.0
    off = channel_mean - mean
    variance = by_group(jnp.sum(weights * spread, axis=0, keepdims=True) + off * off) / 3.0
    scale = 1.0 / jnp.sqrt(variance + 1e-05)
    gain = gain_ref[...]
    steep = scale * gain
    pre_w = jnp.where(place == ONE, shift_ref[...] - mean * steep, weights * steep)
    pre_w = jnp.concatenate(
        [dot_t(perm, part.astype(BF16)) for part in pieces(pre_w, 2)], axis=0
    ).astype(BF16)

    def act_step(c, total):
        taps = digits[pl.ds(c, 3)].reshape(CH, ROWS)
        both = dot(pre_w, taps)
        pre = both[0:CH] + both[CH : 2 * CH]
        sigma = 0.5 * jnp.tanh(0.5 * pre) + 0.5
        act = pre * sigma
        slope = sigma + act * (1.0 - sigma)
        acts[c, 0] = later(act, wide).astype(BF16)
        acts[c, 1] = act.astype(BF16)
        acts[c, 2] = earlier(act, wide).astype(BF16)
        return total + dot_t(taps, (grads[c] * slope).astype(BF16))

    total = lax.fori_loop(0, COLS + 2, act_step, jnp.zeros((CH, CH), F32))
    af[...] = jnp.zeros_like(af)
    af[0:CH, 0:CH] = dot32(total, perm.astype(F32))

    sg[...] = jnp.zeros_like(sg)

    def second_step(c, total):
        value = cot_ref[c]
        sg[:, 0:CH] += dot_t(acts[pl.ds(c, 3)].reshape(9 * CH, ROWS), value)
        return total + dot_t(digits[c + 2], value)

    cot_sum = lax.fori_loop(0, COLS, second_step, jnp.zeros((32, CH), F32))
    af[CH : CH + 8, 0:CH] = cot_sum[8:16]
    sg_send[...] = sg[...].reshape(CHUNKS, 32, 128).astype(BF16)
    for j in range(PLANE - 1):
        af_send[j] = af[unit_row(j) : unit_row(j) + 2, :]
    af_send[PLANE - 1] = jnp.zeros((2, 128), F32)

    for j in range(PLANE):
        @pl.when(q != j)
        def _():
            if j < CHUNKS:
                send(sg_send.at[j], sg_recv.at[q], 3, plane(j)).start()
            send(af_send.at[j], af_recv.at[q], 4, plane(j)).start()
    af_recv[q] = af_send[q]

    @pl.when(q < CHUNKS)
    def _():
        sg_recv[q] = sg_send[q]

    def mixed_step(c, carry):
        out = dot(ahead_w[...], acts[pl.ds(c, 3)].reshape(9 * CH, ROWS))
        lift = dot(lift_w, digits[c + 2])
        lift = (lift[0:CH] + lift[CH : 2 * CH]) + lift[2 * CH : 3 * CH]
        mixed_ref[c] = (lift.astype(BF16).astype(F32) + out).astype(BF16)
        return carry

    lax.fori_loop(0, 6, mixed_step, 0)
    z_send[...] = jnp.zeros_like(z_send)

    @pl.when(q < CHUNKS)
    def _():
        send(sg_send.at[pl.ds(0, CHUNKS - 1)], sg_recv.at[pl.ds(0, CHUNKS - 1)], 3, right).wait_send()
        send(sg_recv.at[pl.ds(0, PLANE - 1)], sg_recv.at[pl.ds(0, PLANE - 1)], 3, right).wait_recv()

        def add(j, total):
            return total + sg_recv[j].astype(F32)

        total = lax.fori_loop(0, PLANE, add, jnp.zeros((32, 128), F32))
        for b in range(BANDS):
            z_send[b, 0:4] = total[4 * b : 4 * b + 4]

    @pl.when(q >= CHUNKS)
    def _():
        send(sg_send, sg_recv.at[pl.ds(0, CHUNKS)], 3, right).wait_send()

    send(af_send.at[pl.ds(0, PLANE - 1)], af_recv.at[pl.ds(0, PLANE - 1)], 4, right).wait()
    af_sum = jnp.sum(af_recv[...], axis=0)
    for b in range(BANDS):
        z_send[b, 4:6] = af_sum

    for j in range(LINE):
        @pl.when(z != j)
        def _():
            send(z_send.at[j % BANDS], z_recv.at[z], 5, line(j)).start()
    z_recv[z] = z_send[band]
    lax.fori_loop(6, 12, mixed_step, 0)
    send(z_recv.at[pl.ds(0, LINE - 1)], z_recv.at[pl.ds(0, LINE - 1)], 5, right).wait()
    ag[q] = jnp.sum(z_recv[...], axis=0)
    for j in range(PLANE):
        @pl.when(q != j)
        def _():
            send(ag.at[q], ag.at[q], 6, plane(j)).start()
    lax.fori_loop(12, COLS, mixed_step, 0)
    send(ag.at[pl.ds(0, PLANE - 1)], ag.at[pl.ds(0, PLANE - 1)], 6, right).wait()

    for j in range(CHUNKS):
        tap = j // 3 % 3 * 3 + j // 9
        second_ref[tap, j % 3 * 4 : j % 3 * 4 + 4, :] = ag[j, 0:4, 0:CH]
    for j in range(PLANE - 1):
        af[unit_row(j) : unit_row(j) + 2, :] = ag[j, 4:6]

    sums = af[0:CH, 0:CH]
    shift_grad = af[ONE : ONE + 1, 0:CH]
    gain_grad = scale * (jnp.sum(weights * sums, axis=0, keepdims=True) - mean * shift_grad)
    shift_out[...] = shift_grad
    gain_out[...] = gain_grad
    count = 3.0 * POSITIONS
    first_mean = by_group(gain * shift_grad) / count
    second_mean = by_group(gain * gain_grad) / count
    standard_sum = scale * (POSITIONS * spread + digit_sum * off)
    grad_sum = scale * (gain * sums - first_mean * digit_sum - second_mean * standard_sum)

    chosen = iota((16, CH), 1) == band * 12 + iota((16, CH), 0)
    proj_band = dot32_t(chosen.astype(F32), proj8)
    back_sum = None
    for dc in range(3):
        for dr in range(3):
            part = grad_sum[dc * 32 + dr * 8 : dc * 32 + dr * 8 + 8]
            first_ref[dr * 3 + dc] = dot32(proj_band, part)[0:12]
            rows = jnp.concatenate(pieces(part, 3) + [no_rows], axis=0).astype(BF16)
            term = dot_t(rows, w1_ref[dr * 3 + dc])
            back_sum = term if back_sum is None else back_sum + term
    back_sum = back_sum[0:8] + back_sum[8:16] + back_sum[16:24] + af[CH : CH + 8, 0:CH]
    proj_out[...] = (back_sum / level)[0:6]


def body(code_ids, projection, first_weight, second_weight, norm_gain, norm_shift, cotangent):
    shape = jax.ShapeDtypeStruct
    vmem = pl.BlockSpec(memory_space=pltpu.VMEM)
    scratch = [
        pltpu.VMEM((COLS, ROWS), F32),
        pltpu.VMEM((2, ROWS), F32), pltpu.VMEM((2, ROWS), F32),
        pltpu.VMEM((2, ROWS), F32), pltpu.VMEM((2, ROWS), F32),
        pltpu.VMEM((COLS + 8, 32, ROWS), BF16),
        pltpu.VMEM((COLS + 4, 3, CH, ROWS), BF16),
        pltpu.VMEM((COLS + 2, 3, CH, ROWS), BF16),
        pltpu.VMEM((COLS + 2, CH, ROWS), F32),
        pltpu.VMEM((9 * CH, CH), BF16), pltpu.VMEM((9 * CH, CH), BF16),
        pltpu.VMEM((CH, 9 * CH), BF16), pltpu.VMEM((CH, 9 * CH), BF16),
        pltpu.VMEM((8, 128), F32), pltpu.VMEM((CH, CH), F32),
        pltpu.VMEM((PLANE, 1, 128), F32), pltpu.VMEM((PLANE, 1, 128), F32),
        pltpu.VMEM((LINE, 1, 128), F32), pltpu.VMEM((PLANE, 1, 128), F32),
        pltpu.VMEM((128, 128), F32),
        pltpu.VMEM((9 * CH, 128), F32),
        pltpu.VMEM((CHUNKS, 32, 128), BF16), pltpu.VMEM((PLANE, 32, 128), BF16),
        pltpu.VMEM((CH + 8, 128), F32),
        pltpu.VMEM((PLANE, 2, 128), F32), pltpu.VMEM((PLANE, 2, 128), F32),
        pltpu.VMEM((BANDS, 8, 128), F32), pltpu.VMEM((LINE, 8, 128), F32),
        pltpu.VMEM((PLANE, 8, 128), F32),
        pltpu.SemaphoreType.DMA((2,)), pltpu.SemaphoreType.DMA((2,)),
        pltpu.SemaphoreType.DMA((7,)), pltpu.SemaphoreType.DMA((7,)),
    ]
    mixed, first, second, gain_grad, shift_grad, proj = pl.pallas_call(
        kernel,
        out_shape=[
            shape((COLS, CH, ROWS), BF16),
            shape((9, 12, CH), F32),
            shape((9, 12, CH), F32),
            shape((1, CH), F32),
            shape((1, CH), F32),
            shape((6, CH), F32),
        ],
        in_specs=[vmem] * 7,
        out_specs=[vmem] * 6,
        scratch_shapes=scratch,
        compiler_params=pltpu.CompilerParams(
            collective_id=0, has_side_effects=True, vmem_limit_bytes=40 * 1024 * 1024
        ),
        cost_estimate=pl.CostEstimate(
            flops=2_500_000_000, bytes_accessed=2_500_000, transcendentals=450_000
        ),
    )(
        code_ids,
        projection,
        first_weight,
        second_weight,
        norm_gain.reshape(1, CH),
        norm_shift.reshape(1, CH),
        cotangent,
    )
    return mixed, first, second, gain_grad.reshape(CH), shift_grad.reshape(CH), proj


def solution(mesh):
    return jax.shard_map(
        body,
        mesh=mesh,
        in_specs=(P("band", None, "face"), P(), P(), P(), P(), P(), P("face", "band", None)),
        out_specs=(
            P("face", "band", None),
            P(None, "band", None),
            P(None, "band", None),
            P(),
            P(),
            P(),
        ),
        check_vma=False,
    )
```

```python
import jax
import jax.numpy as jnp
from jax import lax
from jax.experimental import pallas as pl
from jax.experimental.pallas import tpu as pltpu
from jax.sharding import PartitionSpec as P

MESH = pl.DeviceIdType.MESH
HIGHEST = lax.Precision.HIGHEST
F32, BF16 = jnp.float32, jnp.bfloat16

CH, ROWS, COLS = 96, 256, 16
PLANE, LINE, BANDS = 32, 16, 8
CHUNKS = 27
POSITIONS = float(2**21)
VMEM_BYTES = 64 * 1024 * 1024 - 65536
ONE = 46


def iota(shape, dim):
    return lax.broadcasted_iota(jnp.int32, shape, dim)


def dot(a, b):
    return lax.dot_general(a, b, (((1,), (0,)), ((), ())), preferred_element_type=F32)


def dot_t(a, b):
    return lax.dot_general(a, b, (((1,), (1,)), ((), ())), preferred_element_type=F32)


def dot32(a, b):
    return lax.dot_general(
        a, b, (((1,), (0,)), ((), ())), precision=HIGHEST, preferred_element_type=F32
    )


def dot32_t(a, b):
    return lax.dot_general(
        a, b, (((1,), (1,)), ((), ())), precision=HIGHEST, preferred_element_type=F32
    )


def pieces(value, count):
    parts = []
    for _ in range(count):
        part = value.astype(BF16).astype(F32)
        parts.append(part)
        value = value - part
    return parts


def later(value, lane):
    return jnp.where(lane == 0, 0.0, pltpu.roll(value, 1, 1))


def earlier(value, lane):
    return jnp.where(lane == ROWS - 1, 0.0, pltpu.roll(value, ROWS - 1, 1))


def unit_row(index):
    if index < 27:
        return index // 9 * 32 + index // 3 % 3 * 8 + index % 3 * 2
    return 96 + 2 * (index - 27) if index < 30 else ONE


def kernel(
    code_in, proj_in, w1_in, w2_in, gain_in, shift_in, cot_in,
    mixed_out, first_ref, second_ref, gain_out, shift_out, proj_out,
    code_ref, proj_ref, w1_ref, w2_ref, gain_ref, shift_ref, cot_ref, mixed_ref,
    own, edge_l, edge_r, halo_l, halo_r,
    digits, cots, acts, grads, w2p, w2t, back_w, ahead_w, p8, wt,
    gs, g_rs, g_z, g_ag, g_all,
    sg_send, sg_recv, af, af_send, af_recv, z_send, z_recv, ag,
    in_sem, out_sem, halo_send_sem, halo_recv_sem, send_sem, recv_sem,
):
    arrivals = [
        pltpu.make_async_copy(source, target, in_sem.at[k])
        for k, (source, target) in enumerate(
            [
                (code_in, code_ref), (proj_in, proj_ref), (w1_in, w1_ref), (w2_in, w2_ref),
                (gain_in, gain_ref), (shift_in, shift_ref), (cot_in, cot_ref),
            ]
        )
    ]
    for arrival in arrivals:
        arrival.start()

    face, band = lax.axis_index("face"), lax.axis_index("band")
    core, z_hi, yx = face % 2, face // 2 % 2, face // 4
    q, z = yx * 2 + core, z_hi * BANDS + band

    def plane(j):
        return (j // 2 * 4 + z_hi * 2 + j % 2, band)

    def line(j):
        return (yx * 4 + j // BANDS * 2 + core, j % BANDS)

    left, right = ((face + 63) % 64, band), ((face + 1) % 64, band)

    barrier = pltpu.get_barrier_semaphore()
    for target in (left, right):
        pl.semaphore_signal(barrier, 1, device_id=target, device_id_type=MESH)
    for j in range(PLANE):
        @pl.when(q != j)
        def _():
            pl.semaphore_signal(barrier, 1, device_id=plane(j), device_id_type=MESH)
    for j in range(LINE):
        @pl.when(z != j)
        def _():
            pl.semaphore_signal(barrier, 1, device_id=line(j), device_id_type=MESH)

    def send(src, dst, sem, target):
        return pltpu.make_async_remote_copy(
            src, dst, send_sem.at[sem], recv_sem.at[sem], device_id=target, device_id_type=MESH
        )

    lane = iota((8, ROWS), 1)
    wide = iota((CH, ROWS), 1)

    arrivals[0].wait()
    codes = code_ref[0].astype(F32)
    own[...] = codes
    edge_l[...] = codes[0:2]
    edge_r[...] = codes[COLS - 2 : COLS]

    pl.semaphore_wait(barrier, PLANE - 1 + LINE - 1 + 2)

    to_right = pltpu.make_async_remote_copy(
        edge_r, halo_l, halo_send_sem.at[0], halo_recv_sem.at[0], device_id=right, device_id_type=MESH
    )
    to_left = pltpu.make_async_remote_copy(
        edge_l, halo_r, halo_send_sem.at[1], halo_recv_sem.at[1], device_id=left, device_id_type=MESH
    )
    to_right.start()
    to_left.start()

    for arrival in arrivals[1:]:
        arrival.wait()

    place, channel = iota((CH, CH), 0), iota((CH, CH), 1)
    perm = (channel == place % 32 // 4 * 12 + place // 32 * 4 + place % 4).astype(BF16)
    eye = (channel == place).astype(BF16)
    same_group = (channel // 3 == place // 3).astype(F32)
    for dc in range(3):
        for dr in range(3):
            tap, at = dr * 3 + dc, dc * 3 + dr
            w2p[pl.ds(at * CH, CH), :] = dot(perm, w2_ref[tap]).astype(BF16)
            back = (2 - dc) * 3 + dr
            w2t[pl.ds(back * CH, CH), :] = dot_t(eye, w2p[pl.ds(at * CH, CH), :]).astype(BF16)
    ahead_w[...] = dot_t(eye, w2p[...]).astype(BF16)
    back_w[...] = dot_t(eye, w2t[...]).astype(BF16)

    level = jnp.where(iota((8, 1), 0) < 3, 8.0, 5.0)
    p8[...] = jnp.zeros_like(p8)
    p8[0:6, 0:CH] = proj_ref[...] / level[0:6]
    proj8 = p8[:, 0:CH]
    proj_parts = pieces(proj8, 3)
    proj_rows = jnp.concatenate(proj_parts + [jnp.zeros_like(proj8)], axis=0).astype(BF16)
    for dc in range(3):
        for dr in range(3):
            got = dot(proj_rows, w1_ref[dr * 3 + dc])
            wt[pl.ds(dc * 32 + dr * 8, 8), :] = got[0:8] + got[8:16] + got[16:24]
        wt[pl.ds(dc * 32 + 24, 8), :] = jnp.zeros((8, CH), F32)
    no_rows = jnp.zeros_like(proj8)
    lift_w = jnp.concatenate(
        [
            dot_t(eye, jnp.concatenate([no_rows, part, no_rows, no_rows], axis=0).astype(BF16))
            for part in proj_parts
        ],
        axis=0,
    ).astype(BF16)

    cots[0:2] = jnp.zeros((2, 3, CH, ROWS), BF16)
    cots[COLS + 2 : COLS + 4] = jnp.zeros((2, 3, CH, ROWS), BF16)

    def cot_step(c, carry):
        value = cot_ref[c]
        wider = value.astype(F32)
        cots[c + 2, 0] = earlier(wider, wide).astype(BF16)
        cots[c + 2, 1] = value
        cots[c + 2, 2] = later(wider, wide).astype(BF16)
        return carry

    lax.fori_loop(0, COLS, cot_step, 0)

    to_right.wait()
    to_left.wait()

    index = iota((8, 1), 0)
    stride = jnp.where(
        index == 0, 1.0, jnp.where(index == 1, 8.0, jnp.where(index == 2, 64.0,
        jnp.where(index == 3, 512.0, jnp.where(index == 4, 2560.0, 12800.0)))))
    per_stride, per_level = 1.0 / stride, 1.0 / level
    for c in range(COLS + 4):
        if c < 2:
            row = halo_l[c : c + 1, :]
        elif c < COLS + 2:
            row = own[c - 2 : c - 1, :]
        else:
            row = halo_r[c - COLS - 2 : c - COLS - 1, :]
        quotient = jnp.floor((row + 0.5) * per_stride)
        digit = quotient - level * jnp.floor((quotient + 0.5) * per_level)
        value = jnp.where(index < 6, 2.0 * digit - (level - 1.0), 0.0)
        block = [later(value, lane), jnp.where(index == 6, 1.0, value), earlier(value, lane)]
        digits[c] = jnp.concatenate(block + [jnp.zeros_like(value)], axis=0).astype(BF16)
    digits[COLS + 4 : COLS + 8] = jnp.zeros((4, 32, ROWS), BF16)

    gram = dot_t(
        jnp.concatenate([digits[c + 2] for c in range(COLS)], axis=1),
        jnp.concatenate([digits[c + 2 : c + 6].reshape(128, ROWS) for c in range(COLS)], axis=1),
    )
    for j in range(PLANE):
        gs[j] = gram[j : j + 1]
    for j in range(PLANE):
        @pl.when(q != j)
        def _():
            send(gs.at[j], g_rs.at[q], 0, plane(j)).start()
    g_rs[q] = gs[q]

    def grad_step(step, carry):
        for k in range(6):
            c = step * 6 + k
            grads[c] = dot(back_w[...], cots[pl.ds(c, 3)].reshape(9 * CH, ROWS))
        return carry

    lax.fori_loop(0, 3, grad_step, 0)
    some = send(gs.at[pl.ds(0, PLANE - 1)], g_rs.at[pl.ds(0, PLANE - 1)], 0, right)
    some.wait()
    g_z[z] = jnp.sum(g_rs[...], axis=0)
    for j in range(LINE):
        @pl.when(z != j)
        def _():
            send(g_z.at[z], g_z.at[z], 1, line(j)).start()
    send(g_z.at[pl.ds(0, LINE - 1)], g_z.at[pl.ds(0, LINE - 1)], 1, right).wait()
    g_ag[q] = jnp.sum(g_z[...], axis=0)
    for j in range(PLANE):
        @pl.when(q != j)
        def _():
            send(g_ag.at[q], g_ag.at[q], 2, plane(j)).start()
    send(g_ag.at[pl.ds(0, PLANE - 1)], g_ag.at[pl.ds(0, PLANE - 1)], 2, right).wait()
    for j in range(PLANE):
        g_all[j : j + 1, :] = g_ag[j]
    g_all[PLANE:128, :] = jnp.zeros((128 - PLANE, 128), F32)

    near = g_all[0:32, :]
    flipped = jnp.transpose(g_all[...])
    lane32 = iota((32, 128), 1)
    gram_all = jnp.concatenate(
        [
            near,
            jnp.where(lane32 < 32, flipped[32:64], pltpu.roll(near, 32, 1)),
            jnp.where(
                lane32 < 32,
                flipped[64:96],
                jnp.where(lane32 < 64, pltpu.roll(flipped[32:64], 32, 1), pltpu.roll(near, 64, 1)),
            ),
        ],
        axis=0,
    )[:, 0:CH]
    digit_sum = gram_all[:, ONE : ONE + 1]
    digit_mean = digit_sum / POSITIONS
    covariance = gram_all / POSITIONS - digit_mean * (gram_all[ONE : ONE + 1, :] / POSITIONS)
    weights = wt[...]
    spread = dot32(covariance, weights)

    def by_group(value):
        return dot32(jnp.broadcast_to(value, (8, CH)), same_group)[0:1]

    channel_mean = jnp.sum(weights * digit_mean, axis=0, keepdims=True)
    mean = by_group(channel_mean) / 3.0
    off = channel_mean - mean
    variance = by_group(jnp.sum(weights * spread, axis=0, keepdims=True) + off * off) / 3.0
    scale = 1.0 / jnp.sqrt(variance + 1e-05)
    gain = gain_ref[...]
    steep = scale * gain
    pre_w = jnp.where(place == ONE, shift_ref[...] - mean * steep, weights * steep)
    pre_w = jnp.concatenate(
        [dot_t(perm, part.astype(BF16)) for part in pieces(pre_w, 2)], axis=0
    ).astype(BF16)

    def act_step(step, total):
        for k in range(9):
            c = step * 9 + k
            taps = digits[pl.ds(c, 3)].reshape(CH, ROWS)
            both = dot(pre_w, taps)
            pre = both[0:CH] + both[CH : 2 * CH]
            sigma = 0.5 * jnp.tanh(0.5 * pre) + 0.5
            act = pre * sigma
            slope = sigma + act * (1.0 - sigma)
            acts[c, 0] = later(act, wide).astype(BF16)
            acts[c, 1] = act.astype(BF16)
            acts[c, 2] = earlier(act, wide).astype(BF16)
            total = total + dot_t(taps, (grads[c] * slope).astype(BF16))
        return total

    total = lax.fori_loop(0, 2, act_step, jnp.zeros((CH, CH), F32))
    af[...] = jnp.zeros_like(af)
    af[0:CH, 0:CH] = dot32(total, perm.astype(F32))

    cot_all = jnp.concatenate([cot_ref[c] for c in range(COLS)], axis=1)
    cot_sum = dot_t(jnp.concatenate([digits[c + 2] for c in range(COLS)], axis=1), cot_all)
    af[CH : CH + 8, 0:CH] = cot_sum[8:16]
    for j in range(PLANE - 1):
        af_send[j] = af[unit_row(j) : unit_row(j) + 2, :]
    af_send[PLANE - 1] = jnp.zeros((2, 128), F32)

    for j in range(PLANE):
        @pl.when(q != j)
        def _():
            send(af_send.at[j], af_recv.at[q], 4, plane(j)).start()
    sg_send[:, :, CH:128] = jnp.zeros((CHUNKS, 32, 128 - CH), BF16)
    for dc in range(3):
        taps = [acts[c + dc].reshape(3 * CH, ROWS) for c in range(COLS)]
        got = dot_t(jnp.concatenate(taps, axis=1), cot_all)
        sg_send[9 * dc : 9 * dc + 9, :, 0:CH] = got.reshape(9, 32, CH).astype(BF16)
        for j in range(9 * dc, 9 * dc + 9):
            @pl.when(q != j)
            def _():
                send(sg_send.at[j], sg_recv.at[q], 3, plane(j)).start()
    af_recv[q] = af_send[q]

    @pl.when(q < CHUNKS)
    def _():
        sg_recv[q] = sg_send[q]

    def mixed_step(step, carry):
        for k in range(8):
            c = step * 8 + k
            out = dot(ahead_w[...], acts[pl.ds(c, 3)].reshape(9 * CH, ROWS))
            lift = dot(lift_w, digits[c + 2])
            lift = (lift[0:CH] + lift[CH : 2 * CH]) + lift[2 * CH : 3 * CH]
            mixed_ref[c] = (lift.astype(BF16).astype(F32) + out).astype(BF16)
        return carry

    lax.fori_loop(0, 2, mixed_step, 0)
    departure = pltpu.make_async_copy(mixed_ref, mixed_out, out_sem)
    departure.start()
    z_send[...] = jnp.zeros_like(z_send)

    @pl.when(q < CHUNKS)
    def _():
        send(sg_send.at[pl.ds(0, CHUNKS - 1)], sg_recv.at[pl.ds(0, CHUNKS - 1)], 3, right).wait_send()
        send(sg_recv.at[pl.ds(0, PLANE - 1)], sg_recv.at[pl.ds(0, PLANE - 1)], 3, right).wait_recv()

        def add(j, total):
            return total + sg_recv[j].astype(F32)

        total = lax.fori_loop(0, PLANE, add, jnp.zeros((32, 128), F32))
        for b in range(BANDS):
            z_send[b, 0:4] = total[4 * b : 4 * b + 4]

    @pl.when(q >= CHUNKS)
    def _():
        send(sg_send, sg_recv.at[pl.ds(0, CHUNKS)], 3, right).wait_send()

    send(af_send.at[pl.ds(0, PLANE - 1)], af_recv.at[pl.ds(0, PLANE - 1)], 4, right).wait()
    af_sum = jnp.sum(af_recv[...], axis=0)
    for b in range(BANDS):
        z_send[b, 4:6] = af_sum

    for j in range(LINE):
        @pl.when(z != j)
        def _():
            send(z_send.at[j % BANDS], z_recv.at[z], 5, line(j)).start()
    z_recv[z] = z_send[band]
    send(z_recv.at[pl.ds(0, LINE - 1)], z_recv.at[pl.ds(0, LINE - 1)], 5, right).wait()
    ag[q] = jnp.sum(z_recv[...], axis=0)
    for j in range(PLANE):
        @pl.when(q != j)
        def _():
            send(ag.at[q], ag.at[q], 6, plane(j)).start()
    send(ag.at[pl.ds(0, PLANE - 1)], ag.at[pl.ds(0, PLANE - 1)], 6, right).wait()

    for j in range(CHUNKS):
        tap = j // 3 % 3 * 3 + j // 9
        second_ref[tap, j % 3 * 4 : j % 3 * 4 + 4, :] = ag[j, 0:4, 0:CH]
    for j in range(PLANE - 1):
        af[unit_row(j) : unit_row(j) + 2, :] = ag[j, 4:6]

    sums = af[0:CH, 0:CH]
    shift_grad = af[ONE : ONE + 1, 0:CH]
    gain_grad = scale * (jnp.sum(weights * sums, axis=0, keepdims=True) - mean * shift_grad)
    shift_out[...] = shift_grad
    gain_out[...] = gain_grad
    count = 3.0 * POSITIONS
    first_mean = by_group(gain * shift_grad) / count
    second_mean = by_group(gain * gain_grad) / count
    standard_sum = scale * (POSITIONS * spread + digit_sum * off)
    grad_sum = scale * (gain * sums - first_mean * digit_sum - second_mean * standard_sum)

    chosen = iota((16, CH), 1) == band * 12 + iota((16, CH), 0)
    proj_band = dot32_t(chosen.astype(F32), proj8)
    back_sum = None
    for dc in range(3):
        for dr in range(3):
            part = grad_sum[dc * 32 + dr * 8 : dc * 32 + dr * 8 + 8]
            first_ref[dr * 3 + dc] = dot32(proj_band, part)[0:12]
            rows = jnp.concatenate(pieces(part, 3) + [no_rows], axis=0).astype(BF16)
            term = dot_t(rows, w1_ref[dr * 3 + dc])
            back_sum = term if back_sum is None else back_sum + term
    back_sum = back_sum[0:8] + back_sum[8:16] + back_sum[16:24] + af[CH : CH + 8, 0:CH]
    proj_out[...] = (back_sum / level)[0:6]
    departure.wait()


def write_out(*refs):
    sources, targets, held = refs[0:6], refs[6:12], refs[12:18]
    in_sem, out_sem = refs[18], refs[19]
    parts = [(0, pl.ds(4 * k, 4)) for k in range(4)] + [(k, None) for k in range(1, 6)]

    def view(group, part):
        which, rows = part
        return group[which] if rows is None else group[which].at[rows]

    ins = [
        pltpu.make_async_copy(view(sources, part), view(held, part), in_sem.at[k])
        for k, part in enumerate(parts)
    ]
    outs = [
        pltpu.make_async_copy(view(held, part), view(targets, part), out_sem.at[k])
        for k, part in enumerate(parts)
    ]
    for copy in ins:
        copy.start()
    for arrived, copy in zip(ins, outs):
        arrived.wait()
        copy.start()
    for copy in outs:
        copy.wait()


def body(code_ids, projection, first_weight, second_weight, norm_gain, norm_shift, cotangent):
    shape = jax.ShapeDtypeStruct
    vmem = pl.BlockSpec(memory_space=pltpu.VMEM)
    anywhere = pl.BlockSpec(memory_space=pltpu.HBM)
    operands = [
        jnp.swapaxes(code_ids, 1, 2),
        projection,
        first_weight,
        second_weight,
        norm_gain.reshape(1, CH),
        norm_shift.reshape(1, CH),
        cotangent,
    ]
    scratch = [pltpu.VMEM(operand.shape, operand.dtype) for operand in operands] + [
        pltpu.VMEM((COLS, CH, ROWS), BF16),
        pltpu.VMEM((COLS, ROWS), F32),
        pltpu.VMEM((2, ROWS), F32), pltpu.VMEM((2, ROWS), F32),
        pltpu.VMEM((2, ROWS), F32), pltpu.VMEM((2, ROWS), F32),
        pltpu.VMEM((COLS + 8, 32, ROWS), BF16),
        pltpu.VMEM((COLS + 4, 3, CH, ROWS), BF16),
        pltpu.VMEM((COLS + 2, 3, CH, ROWS), BF16),
        pltpu.VMEM((COLS + 2, CH, ROWS), F32),
        pltpu.VMEM((9 * CH, CH), BF16), pltpu.VMEM((9 * CH, CH), BF16),
        pltpu.VMEM((CH, 9 * CH), BF16), pltpu.VMEM((CH, 9 * CH), BF16),
        pltpu.VMEM((8, 128), F32), pltpu.VMEM((CH, CH), F32),
        pltpu.VMEM((PLANE, 1, 128), F32), pltpu.VMEM((PLANE, 1, 128), F32),
        pltpu.VMEM((LINE, 1, 128), F32), pltpu.VMEM((PLANE, 1, 128), F32),
        pltpu.VMEM((128, 128), F32),
        pltpu.VMEM((CHUNKS, 32, 128), BF16), pltpu.VMEM((PLANE, 32, 128), BF16),
        pltpu.VMEM((CH + 8, 128), F32),
        pltpu.VMEM((PLANE, 2, 128), F32), pltpu.VMEM((PLANE, 2, 128), F32),
        pltpu.VMEM((BANDS, 8, 128), F32), pltpu.VMEM((LINE, 8, 128), F32),
        pltpu.VMEM((PLANE, 8, 128), F32),
        pltpu.SemaphoreType.DMA((7,)), pltpu.SemaphoreType.DMA,
        pltpu.SemaphoreType.DMA((2,)), pltpu.SemaphoreType.DMA((2,)),
        pltpu.SemaphoreType.DMA((7,)), pltpu.SemaphoreType.DMA((7,)),
    ]
    outputs = [
        shape((COLS, CH, ROWS), BF16),
        shape((9, 12, CH), F32),
        shape((9, 12, CH), F32),
        shape((1, CH), F32),
        shape((1, CH), F32),
        shape((6, CH), F32),
    ]
    results = pl.pallas_call(
        kernel,
        out_shape=outputs,
        in_specs=[anywhere] * 7,
        out_specs=[anywhere] + [vmem] * 5,
        scratch_shapes=scratch,
        compiler_params=pltpu.CompilerParams(
            collective_id=0, has_side_effects=True, vmem_limit_bytes=VMEM_BYTES
        ),
        cost_estimate=pl.CostEstimate(
            flops=2_500_000_000, bytes_accessed=2_500_000, transcendentals=450_000
        ),
    )(*operands)
    mixed, first, second, gain_grad, shift_grad, proj = pl.pallas_call(
        write_out,
        out_shape=outputs,
        in_specs=[anywhere] * 6,
        out_specs=[anywhere] * 6,
        scratch_shapes=[pltpu.VMEM(output.shape, output.dtype) for output in outputs]
        + [pltpu.SemaphoreType.DMA((9,)), pltpu.SemaphoreType.DMA((9,))],
        compiler_params=pltpu.CompilerParams(vmem_limit_bytes=VMEM_BYTES),
    )(*results)
    return mixed, first, second, gain_grad.reshape(CH), shift_grad.reshape(CH), proj


def solution(mesh):
    return jax.shard_map(
        body,
        mesh=mesh,
        in_specs=(P("band", None, "face"), P(), P(), P(), P(), P(), P("face", "band", None)),
        out_specs=(
            P("face", "band", None),
            P(None, "band", None),
            P(None, "band", None),
            P(),
            P(),
            P(),
        ),
        check_vma=False,
    )
```

```python
import jax
import jax.numpy as jnp
from jax import lax
from jax.experimental import pallas as pl
from jax.experimental.pallas import tpu as pltpu
from jax.sharding import PartitionSpec as P

MESH = pl.DeviceIdType.MESH
HIGHEST = lax.Precision.HIGHEST
F32, BF16 = jnp.float32, jnp.bfloat16

CH, ROWS, COLS = 96, 256, 16
PLANE, LINE, BANDS = 32, 16, 8
CHUNKS = 27
POSITIONS = float(2**21)


def hops(step, ring):
    return min(step, ring - step)


PLANE_OFFSETS = sorted(
    [(dy, dx, dc) for dy in range(4) for dx in range(4) for dc in range(2) if dy + dx + dc > 0],
    key=lambda step: -4 * hops(step[0], 4) - 4 * hops(step[1], 4) - step[2],
)
LINE_OFFSETS = sorted(range(1, LINE), key=lambda step: -hops(step, LINE))
VMEM_BYTES = 64 * 1024 * 1024 - 65536
ONE = 46


def iota(shape, dim):
    return lax.broadcasted_iota(jnp.int32, shape, dim)


def dot(a, b):
    return lax.dot_general(a, b, (((1,), (0,)), ((), ())), preferred_element_type=F32)


def dot_t(a, b):
    return lax.dot_general(a, b, (((1,), (1,)), ((), ())), preferred_element_type=F32)


def dot32(a, b):
    return lax.dot_general(
        a, b, (((1,), (0,)), ((), ())), precision=HIGHEST, preferred_element_type=F32
    )


def dot32_t(a, b):
    return lax.dot_general(
        a, b, (((1,), (1,)), ((), ())), precision=HIGHEST, preferred_element_type=F32
    )


def pieces(value, count):
    parts = []
    for _ in range(count):
        part = value.astype(BF16).astype(F32)
        parts.append(part)
        value = value - part
    return parts


def later(value, lane):
    return jnp.where(lane == 0, 0.0, pltpu.roll(value, 1, 1))


def earlier(value, lane):
    return jnp.where(lane == ROWS - 1, 0.0, pltpu.roll(value, ROWS - 1, 1))


def unit_row(index):
    if index < 27:
        return index // 9 * 32 + index // 3 % 3 * 8 + index % 3 * 2
    return 96 + 2 * (index - 27) if index < 30 else ONE


def kernel(
    code_in, proj_in, w1_in, w2_in, gain_in, shift_in, cot_in,
    mixed_out, first_ref, second_ref, gain_out, shift_out, proj_out,
    code_ref, proj_ref, w1_ref, w2_ref, gain_ref, shift_ref, cot_ref, mixed_ref,
    own, edge_l, edge_r, halo_l, halo_r, mid_l, mid_r, seam,
    digits, cots, acts, grads, w2p, w2t, back_w, ahead_w, p8, wt,
    gs, g_rs, g_z, g_ag, g_all,
    sg_send, sg_recv, af, af_send, af_recv, z_send, z_recv, ag,
    in_sem, out_sem, halo_send_sem, halo_recv_sem, send_sem, recv_sem,
):
    face, band = lax.axis_index("face"), lax.axis_index("band")
    core, z_hi, yx = face % 2, face // 2 % 2, face // 4
    y, x = yx // 4, yx % 4
    q, z = yx * 2 + core, z_hi * BANDS + band

    def plane(j):
        return (j // 2 * 4 + z_hi * 2 + j % 2, band)

    def line(j):
        return (yx * 4 + j // BANDS * 2 + core, j % BANDS)

    mates = [
        ((y + dy) % 4 * 4 + (x + dx) % 4) * 2 + (core + dc) % 2 for dy, dx, dc in PLANE_OFFSETS
    ]
    others = [(z + dz) % LINE for dz in LINE_OFFSETS]

    left, right = ((face + 63) % 64, band), ((face + 1) % 64, band)

    def half_way(seam_face):
        there = (seam_face // 2 % 2 * BANDS + band + 4) % LINE
        return (seam_face // 4 * 4 + there // BANDS * 2 + 1, there % BANDS)

    from_z = (z + 12) % LINE
    from_right = ((yx * 4 + from_z // BANDS * 2 + 2) % 64, from_z % BANDS)

    barrier = pltpu.get_barrier_semaphore()
    for target in (left, right):
        pl.semaphore_signal(barrier, 1, device_id=target, device_id_type=MESH)
    @pl.when(core == 1)
    def _():
        pl.semaphore_signal(barrier, 1, device_id=from_right, device_id_type=MESH)

    for j in others:
        pl.semaphore_signal(barrier, 1, device_id=line(j), device_id_type=MESH)
    for j in mates:
        pl.semaphore_signal(barrier, 1, device_id=plane(j), device_id_type=MESH)

    arrivals = [
        pltpu.make_async_copy(source, target, in_sem.at[k])
        for k, (source, target) in enumerate(
            [
                (code_in, code_ref), (proj_in, proj_ref), (w1_in, w1_ref), (w2_in, w2_ref),
                (gain_in, gain_ref), (shift_in, shift_ref), (cot_in, cot_ref),
            ]
        )
    ]
    for arrival in arrivals:
        arrival.start()

    def send(src, dst, sem, target):
        return pltpu.make_async_remote_copy(
            src, dst, send_sem.at[sem], recv_sem.at[sem], device_id=target, device_id_type=MESH
        )

    lane = iota((8, ROWS), 1)
    wide = iota((CH, ROWS), 1)

    arrivals[0].wait()
    codes = code_ref[0].astype(F32)
    own[...] = codes
    edge_l[...] = codes[0:2]
    edge_r[...] = codes[COLS - 2 : COLS]

    pl.semaphore_wait(barrier, PLANE - 1 + LINE - 1 + 2 + 1 - core)

    to_right = pltpu.make_async_remote_copy(
        edge_r, halo_l, halo_send_sem.at[0], halo_recv_sem.at[0], device_id=right, device_id_type=MESH
    )
    to_left = pltpu.make_async_remote_copy(
        edge_l, halo_r, halo_send_sem.at[1], halo_recv_sem.at[1], device_id=left, device_id_type=MESH
    )
    mid_right = pltpu.make_async_remote_copy(
        edge_r, mid_l, halo_send_sem.at[2], halo_recv_sem.at[2],
        device_id=half_way(face), device_id_type=MESH,
    )
    mid_left = pltpu.make_async_remote_copy(
        edge_l, mid_r, halo_send_sem.at[3], halo_recv_sem.at[3],
        device_id=half_way((face + 63) % 64), device_id_type=MESH,
    )

    @pl.when(core == 1)
    def _():
        mid_right.start()

    @pl.when(core == 0)
    def _():
        mid_left.start()

    to_left.start()
    to_right.start()

    for arrival in arrivals[1:]:
        arrival.wait()

    place, channel = iota((CH, CH), 0), iota((CH, CH), 1)
    perm = (channel == place % 32 // 4 * 12 + place // 32 * 4 + place % 4).astype(BF16)
    eye = (channel == place).astype(BF16)
    same_group = (channel // 3 == place // 3).astype(F32)
    for dc in range(3):
        for dr in range(3):
            tap, at = dr * 3 + dc, dc * 3 + dr
            w2p[pl.ds(at * CH, CH), :] = dot(perm, w2_ref[tap]).astype(BF16)
            back = (2 - dc) * 3 + dr
            w2t[pl.ds(back * CH, CH), :] = dot_t(eye, w2p[pl.ds(at * CH, CH), :]).astype(BF16)
    ahead_w[...] = dot_t(eye, w2p[...]).astype(BF16)
    back_w[...] = dot_t(eye, w2t[...]).astype(BF16)

    level = jnp.where(iota((8, 1), 0) < 3, 8.0, 5.0)
    p8[...] = jnp.zeros_like(p8)
    p8[0:6, 0:CH] = proj_ref[...] / level[0:6]
    proj8 = p8[:, 0:CH]
    proj_parts = pieces(proj8, 3)
    proj_rows = jnp.concatenate(proj_parts + [jnp.zeros_like(proj8)], axis=0).astype(BF16)
    for dc in range(3):
        for dr in range(3):
            got = dot(proj_rows, w1_ref[dr * 3 + dc])
            wt[pl.ds(dc * 32 + dr * 8, 8), :] = got[0:8] + got[8:16] + got[16:24]
        wt[pl.ds(dc * 32 + 24, 8), :] = jnp.zeros((8, CH), F32)
    no_rows = jnp.zeros_like(proj8)
    lift_w = jnp.concatenate(
        [
            dot_t(eye, jnp.concatenate([no_rows, part, no_rows, no_rows], axis=0).astype(BF16))
            for part in proj_parts
        ],
        axis=0,
    ).astype(BF16)

    cots[0:2] = jnp.zeros((2, 3, CH, ROWS), BF16)
    cots[COLS + 2 : COLS + 4] = jnp.zeros((2, 3, CH, ROWS), BF16)

    def cot_step(c, carry):
        value = cot_ref[c]
        wider = value.astype(F32)
        cots[c + 2, 0] = earlier(wider, wide).astype(BF16)
        cots[c + 2, 1] = value
        cots[c + 2, 2] = later(wider, wide).astype(BF16)
        return carry

    lax.fori_loop(0, COLS, cot_step, 0)

    index = iota((8, 1), 0)
    stride = jnp.where(
        index == 0, 1.0, jnp.where(index == 1, 8.0, jnp.where(index == 2, 64.0,
        jnp.where(index == 3, 512.0, jnp.where(index == 4, 2560.0, 12800.0)))))
    per_stride, per_level = 1.0 / stride, 1.0 / level

    def decode(row):
        quotient = jnp.floor((row + 0.5) * per_stride)
        digit = quotient - level * jnp.floor((quotient + 0.5) * per_level)
        value = jnp.where(index < 6, 2.0 * digit - (level - 1.0), 0.0)
        block = [later(value, lane), jnp.where(index == 6, 1.0, value), earlier(value, lane)]
        return jnp.concatenate(block + [jnp.zeros_like(value)], axis=0).astype(BF16)

    for c in range(COLS):
        digits[c + 2] = decode(own[c : c + 1, :])

    @pl.when(core == 0)
    def _():
        to_left.wait_recv()
        seam[0:2, :] = own[COLS - 2 : COLS, :]
        seam[2:4, :] = halo_r[...]

    @pl.when(core == 1)
    def _():
        mid_right.wait_recv()
        mid_left.wait_recv()
        seam[0:2, :] = mid_l[...]
        seam[2:4, :] = mid_r[...]

    beside = [decode(seam[c : c + 1, :]) for c in range(4)]

    none = jnp.zeros((32, ROWS), BF16)

    def ahead(c):
        return jnp.concatenate(
            [digits[c + 2 + d] if c + d < COLS else none for d in range(3)] + [none], axis=0
        )

    gram = dot_t(
        jnp.concatenate([digits[c + 2] for c in range(COLS)] + beside[0:2], axis=1),
        jnp.concatenate(
            [ahead(c) for c in range(COLS)]
            + [
                jnp.concatenate([none, none, beside[2], none], axis=0),
                jnp.concatenate([none, beside[2], beside[3], none], axis=0),
            ],
            axis=1,
        ),
    )
    for j in range(PLANE):
        gs[j] = gram[j : j + 1]
    for j in mates:
        send(gs.at[j], g_rs.at[q], 0, plane(j)).start()
    g_rs[q] = gs[q]

    @pl.when(core == 1)
    def _():
        to_left.wait_recv()
        mid_right.wait_send()

    @pl.when(core == 0)
    def _():
        mid_left.wait_send()

    to_left.wait_send()
    to_right.wait()
    for c in range(2):
        digits[c] = decode(halo_l[c : c + 1, :])
        digits[COLS + 2 + c] = decode(halo_r[c : c + 1, :])

    def grad_step(step, carry):
        for k in range(6):
            c = step * 6 + k
            grads[c] = dot(back_w[...], cots[pl.ds(c, 3)].reshape(9 * CH, ROWS))
        return carry

    lax.fori_loop(0, 3, grad_step, 0)
    some = send(gs.at[pl.ds(0, PLANE - 1)], g_rs.at[pl.ds(0, PLANE - 1)], 0, right)
    some.wait()
    g_z[z] = jnp.sum(g_rs[...], axis=0)
    for j in others:
        send(g_z.at[z], g_z.at[z], 1, line(j)).start()
    send(g_z.at[pl.ds(0, LINE - 1)], g_z.at[pl.ds(0, LINE - 1)], 1, right).wait()
    g_ag[q] = jnp.sum(g_z[...], axis=0)
    for j in mates:
        send(g_ag.at[q], g_ag.at[q], 2, plane(j)).start()
    send(g_ag.at[pl.ds(0, PLANE - 1)], g_ag.at[pl.ds(0, PLANE - 1)], 2, right).wait()
    for j in range(PLANE):
        g_all[j : j + 1, :] = g_ag[j]
    g_all[PLANE:128, :] = jnp.zeros((128 - PLANE, 128), F32)

    near = g_all[0:32, :]
    flipped = jnp.transpose(g_all[...])
    lane32 = iota((32, 128), 1)
    gram_all = jnp.concatenate(
        [
            near,
            jnp.where(lane32 < 32, flipped[32:64], pltpu.roll(near, 32, 1)),
            jnp.where(
                lane32 < 32,
                flipped[64:96],
                jnp.where(lane32 < 64, pltpu.roll(flipped[32:64], 32, 1), pltpu.roll(near, 64, 1)),
            ),
        ],
        axis=0,
    )[:, 0:CH]
    digit_sum = gram_all[:, ONE : ONE + 1]
    digit_mean = digit_sum / POSITIONS
    covariance = gram_all / POSITIONS - digit_mean * (gram_all[ONE : ONE + 1, :] / POSITIONS)
    weights = wt[...]
    spread = dot32(covariance, weights)

    def by_group(value):
        return dot32(jnp.broadcast_to(value, (8, CH)), same_group)[0:1]

    channel_mean = jnp.sum(weights * digit_mean, axis=0, keepdims=True)
    mean = by_group(channel_mean) / 3.0
    off = channel_mean - mean
    variance = by_group(jnp.sum(weights * spread, axis=0, keepdims=True) + off * off) / 3.0
    scale = 1.0 / jnp.sqrt(variance + 1e-05)
    gain = gain_ref[...]
    steep = scale * gain
    pre_w = jnp.where(place == ONE, shift_ref[...] - mean * steep, weights * steep)
    pre_w = jnp.concatenate(
        [dot_t(perm, part.astype(BF16)) for part in pieces(pre_w, 2)], axis=0
    ).astype(BF16)

    def act_step(step, total):
        for k in range(9):
            c = step * 9 + k
            taps = digits[pl.ds(c, 3)].reshape(CH, ROWS)
            both = dot(pre_w, taps)
            pre = both[0:CH] + both[CH : 2 * CH]
            sigma = 0.5 * jnp.tanh(0.5 * pre) + 0.5
            act = pre * sigma
            slope = sigma + act * (1.0 - sigma)
            acts[c, 0] = later(act, wide).astype(BF16)
            acts[c, 1] = act.astype(BF16)
            acts[c, 2] = earlier(act, wide).astype(BF16)
            total = total + dot_t(taps, (grads[c] * slope).astype(BF16))
        return total

    total = lax.fori_loop(0, 2, act_step, jnp.zeros((CH, CH), F32))
    af[...] = jnp.zeros_like(af)
    af[0:CH, 0:CH] = dot32(total, perm.astype(F32))

    cot_all = jnp.concatenate([cot_ref[c] for c in range(COLS)], axis=1)
    cot_sum = dot_t(jnp.concatenate([digits[c + 2] for c in range(COLS)], axis=1), cot_all)
    af[CH : CH + 8, 0:CH] = cot_sum[8:16]
    for j in range(PLANE - 1):
        af_send[j] = af[unit_row(j) : unit_row(j) + 2, :]
    af_send[PLANE - 1] = jnp.zeros((2, 128), F32)

    for j in mates:
        send(af_send.at[j], af_recv.at[q], 4, plane(j)).start()
    sg_send[:, :, CH:128] = jnp.zeros((CHUNKS, 32, 128 - CH), BF16)
    for dc in range(3):
        taps = [acts[c + dc].reshape(3 * CH, ROWS) for c in range(COLS)]
        got = dot_t(jnp.concatenate(taps, axis=1), cot_all)
        sg_send[9 * dc : 9 * dc + 9, :, 0:CH] = got.reshape(9, 32, CH).astype(BF16)
        for j in range(9 * dc, 9 * dc + 9):
            @pl.when(q != j)
            def _():
                send(sg_send.at[j], sg_recv.at[q], 3, plane(j)).start()
    af_recv[q] = af_send[q]

    @pl.when(q < CHUNKS)
    def _():
        sg_recv[q] = sg_send[q]

    def mixed_step(step, carry):
        for k in range(8):
            c = step * 8 + k
            out = dot(ahead_w[...], acts[pl.ds(c, 3)].reshape(9 * CH, ROWS))
            lift = dot(lift_w, digits[c + 2])
            lift = (lift[0:CH] + lift[CH : 2 * CH]) + lift[2 * CH : 3 * CH]
            mixed_ref[c] = (lift.astype(BF16).astype(F32) + out).astype(BF16)
        return carry

    lax.fori_loop(0, 2, mixed_step, 0)
    departure = pltpu.make_async_copy(mixed_ref, mixed_out, out_sem)
    departure.start()
    z_send[...] = jnp.zeros_like(z_send)

    @pl.when(q < CHUNKS)
    def _():
        send(sg_send.at[pl.ds(0, CHUNKS - 1)], sg_recv.at[pl.ds(0, CHUNKS - 1)], 3, right).wait_send()
        send(sg_recv.at[pl.ds(0, PLANE - 1)], sg_recv.at[pl.ds(0, PLANE - 1)], 3, right).wait_recv()

        def add(j, total):
            return total + sg_recv[j].astype(F32)

        total = lax.fori_loop(0, PLANE, add, jnp.zeros((32, 128), F32))
        for b in range(BANDS):
            z_send[b, 0:4] = total[4 * b : 4 * b + 4]

    @pl.when(q >= CHUNKS)
    def _():
        send(sg_send, sg_recv.at[pl.ds(0, CHUNKS)], 3, right).wait_send()

    send(af_send.at[pl.ds(0, PLANE - 1)], af_recv.at[pl.ds(0, PLANE - 1)], 4, right).wait()
    af_sum = jnp.sum(af_recv[...], axis=0)
    for b in range(BANDS):
        z_send[b, 4:6] = af_sum

    for j in others:
        send(z_send.at[j % BANDS], z_recv.at[z], 5, line(j)).start()
    z_recv[z] = z_send[band]
    send(z_recv.at[pl.ds(0, LINE - 1)], z_recv.at[pl.ds(0, LINE - 1)], 5, right).wait()
    ag[q] = jnp.sum(z_recv[...], axis=0)
    for j in mates:
        send(ag.at[q], ag.at[q], 6, plane(j)).start()
    send(ag.at[pl.ds(0, PLANE - 1)], ag.at[pl.ds(0, PLANE - 1)], 6, right).wait()

    for j in range(CHUNKS):
        tap = j // 3 % 3 * 3 + j // 9
        second_ref[tap, j % 3 * 4 : j % 3 * 4 + 4, :] = ag[j, 0:4, 0:CH]
    for j in range(PLANE - 1):
        af[unit_row(j) : unit_row(j) + 2, :] = ag[j, 4:6]

    sums = af[0:CH, 0:CH]
    shift_grad = af[ONE : ONE + 1, 0:CH]
    gain_grad = scale * (jnp.sum(weights * sums, axis=0, keepdims=True) - mean * shift_grad)
    shift_out[...] = shift_grad
    gain_out[...] = gain_grad
    count = 3.0 * POSITIONS
    first_mean = by_group(gain * shift_grad) / count
    second_mean = by_group(gain * gain_grad) / count
    standard_sum = scale * (POSITIONS * spread + digit_sum * off)
    grad_sum = scale * (gain * sums - first_mean * digit_sum - second_mean * standard_sum)

    chosen = iota((16, CH), 1) == band * 12 + iota((16, CH), 0)
    proj_band = dot32_t(chosen.astype(F32), proj8)
    back_sum = None
    for dc in range(3):
        for dr in range(3):
            part = grad_sum[dc * 32 + dr * 8 : dc * 32 + dr * 8 + 8]
            first_ref[dr * 3 + dc] = dot32(proj_band, part)[0:12]
            rows = jnp.concatenate(pieces(part, 3) + [no_rows], axis=0).astype(BF16)
            term = dot_t(rows, w1_ref[dr * 3 + dc])
            back_sum = term if back_sum is None else back_sum + term
    back_sum = back_sum[0:8] + back_sum[8:16] + back_sum[16:24] + af[CH : CH + 8, 0:CH]
    proj_out[...] = (back_sum / level)[0:6]
    departure.wait()


def write_out(*refs):
    sources, targets, held = refs[0:6], refs[6:12], refs[12:18]
    in_sem, out_sem = refs[18], refs[19]
    parts = [(0, pl.ds(4 * k, 4)) for k in range(4)] + [(k, None) for k in range(1, 6)]

    def view(group, part):
        which, rows = part
        return group[which] if rows is None else group[which].at[rows]

    ins = [
        pltpu.make_async_copy(view(sources, part), view(held, part), in_sem.at[k])
        for k, part in enumerate(parts)
    ]
    outs = [
        pltpu.make_async_copy(view(held, part), view(targets, part), out_sem.at[k])
        for k, part in enumerate(parts)
    ]
    for copy in ins:
        copy.start()
    for arrived, copy in zip(ins, outs):
        arrived.wait()
        copy.start()
    for copy in outs:
        copy.wait()


def body(code_ids, projection, first_weight, second_weight, norm_gain, norm_shift, cotangent):
    shape = jax.ShapeDtypeStruct
    vmem = pl.BlockSpec(memory_space=pltpu.VMEM)
    anywhere = pl.BlockSpec(memory_space=pltpu.HBM)
    operands = [
        jnp.swapaxes(code_ids, 1, 2),
        projection,
        first_weight,
        second_weight,
        norm_gain.reshape(1, CH),
        norm_shift.reshape(1, CH),
        cotangent,
    ]
    scratch = [pltpu.VMEM(operand.shape, operand.dtype) for operand in operands] + [
        pltpu.VMEM((COLS, CH, ROWS), BF16),
        pltpu.VMEM((COLS, ROWS), F32),
        pltpu.VMEM((2, ROWS), F32), pltpu.VMEM((2, ROWS), F32),
        pltpu.VMEM((2, ROWS), F32), pltpu.VMEM((2, ROWS), F32),
        pltpu.VMEM((2, ROWS), F32), pltpu.VMEM((2, ROWS), F32), pltpu.VMEM((4, ROWS), F32),
        pltpu.VMEM((COLS + 4, 32, ROWS), BF16),
        pltpu.VMEM((COLS + 4, 3, CH, ROWS), BF16),
        pltpu.VMEM((COLS + 2, 3, CH, ROWS), BF16),
        pltpu.VMEM((COLS + 2, CH, ROWS), F32),
        pltpu.VMEM((9 * CH, CH), BF16), pltpu.VMEM((9 * CH, CH), BF16),
        pltpu.VMEM((CH, 9 * CH), BF16), pltpu.VMEM((CH, 9 * CH), BF16),
        pltpu.VMEM((8, 128), F32), pltpu.VMEM((CH, CH), F32),
        pltpu.VMEM((PLANE, 1, 128), F32), pltpu.VMEM((PLANE, 1, 128), F32),
        pltpu.VMEM((LINE, 1, 128), F32), pltpu.VMEM((PLANE, 1, 128), F32),
        pltpu.VMEM((128, 128), F32),
        pltpu.VMEM((CHUNKS, 32, 128), BF16), pltpu.VMEM((PLANE, 32, 128), BF16),
        pltpu.VMEM((CH + 8, 128), F32),
        pltpu.VMEM((PLANE, 2, 128), F32), pltpu.VMEM((PLANE, 2, 128), F32),
        pltpu.VMEM((BANDS, 8, 128), F32), pltpu.VMEM((LINE, 8, 128), F32),
        pltpu.VMEM((PLANE, 8, 128), F32),
        pltpu.SemaphoreType.DMA((7,)), pltpu.SemaphoreType.DMA,
        pltpu.SemaphoreType.DMA((4,)), pltpu.SemaphoreType.DMA((4,)),
        pltpu.SemaphoreType.DMA((7,)), pltpu.SemaphoreType.DMA((7,)),
    ]
    outputs = [
        shape((COLS, CH, ROWS), BF16),
        shape((9, 12, CH), F32),
        shape((9, 12, CH), F32),
        shape((1, CH), F32),
        shape((1, CH), F32),
        shape((6, CH), F32),
    ]
    results = pl.pallas_call(
        kernel,
        out_shape=outputs,
        in_specs=[anywhere] * 7,
        out_specs=[anywhere] + [vmem] * 5,
        scratch_shapes=scratch,
        compiler_params=pltpu.CompilerParams(
            collective_id=0, has_side_effects=True, vmem_limit_bytes=VMEM_BYTES
        ),
        cost_estimate=pl.CostEstimate(
            flops=2_500_000_000, bytes_accessed=2_500_000, transcendentals=450_000
        ),
    )(*operands)
    mixed, first, second, gain_grad, shift_grad, proj = pl.pallas_call(
        write_out,
        out_shape=outputs,
        in_specs=[anywhere] * 6,
        out_specs=[anywhere] * 6,
        scratch_shapes=[pltpu.VMEM(output.shape, output.dtype) for output in outputs]
        + [pltpu.SemaphoreType.DMA((9,)), pltpu.SemaphoreType.DMA((9,))],
        compiler_params=pltpu.CompilerParams(vmem_limit_bytes=VMEM_BYTES),
    )(*results)
    return mixed, first, second, gain_grad.reshape(CH), shift_grad.reshape(CH), proj


def solution(mesh):
    return jax.shard_map(
        body,
        mesh=mesh,
        in_specs=(P("band", None, "face"), P(), P(), P(), P(), P(), P("face", "band", None)),
        out_specs=(
            P("face", "band", None),
            P(None, "band", None),
            P(None, "band", None),
            P(),
            P(),
            P(),
        ),
        check_vma=False,
    )
```

```python
import jax
import jax.numpy as jnp
from jax import lax
from jax.experimental import pallas as pl
from jax.experimental.pallas import tpu as pltpu
from jax.sharding import PartitionSpec as P

MESH = pl.DeviceIdType.MESH
HIGHEST = lax.Precision.HIGHEST
F32, BF16 = jnp.float32, jnp.bfloat16

CH, ROWS, COLS = 96, 256, 16
PLANE, LINE, BANDS = 32, 16, 8
CHUNKS = 27
POSITIONS = float(2**21)


def hops(step, ring):
    return min(step, ring - step)


PLANE_OFFSETS = sorted(
    [(dy, dx, dc) for dy in range(4) for dx in range(4) for dc in range(2) if dy + dx + dc > 0],
    key=lambda step: -4 * hops(step[0], 4) - 4 * hops(step[1], 4) - step[2],
)
LINE_OFFSETS = sorted(range(1, LINE), key=lambda step: -hops(step, LINE))
VMEM_BYTES = 64 * 1024 * 1024 - 65536
ONE = 46


def iota(shape, dim):
    return lax.broadcasted_iota(jnp.int32, shape, dim)


def dot(a, b):
    return lax.dot_general(a, b, (((1,), (0,)), ((), ())), preferred_element_type=F32)


def dot_t(a, b):
    return lax.dot_general(a, b, (((1,), (1,)), ((), ())), preferred_element_type=F32)


def dot32(a, b):
    return lax.dot_general(
        a, b, (((1,), (0,)), ((), ())), precision=HIGHEST, preferred_element_type=F32
    )


def dot32_t(a, b):
    return lax.dot_general(
        a, b, (((1,), (1,)), ((), ())), precision=HIGHEST, preferred_element_type=F32
    )


def pieces(value, count):
    parts = []
    for _ in range(count):
        part = value.astype(BF16).astype(F32)
        parts.append(part)
        value = value - part
    return parts


def later(value, lane):
    return jnp.where(lane == 0, 0.0, pltpu.roll(value, 1, 1))


def earlier(value, lane):
    return jnp.where(lane == ROWS - 1, 0.0, pltpu.roll(value, ROWS - 1, 1))


def unit_row(index):
    if index < 27:
        return index // 9 * 32 + index // 3 % 3 * 8 + index % 3 * 2
    return 96 + 2 * (index - 27) if index < 30 else ONE


def kernel(
    code_in, proj_in, w1_in, w2_in, gain_in, shift_in, cot_in,
    mixed_out, first_ref, second_ref, gain_out, shift_out, proj_out,
    code_ref, proj_ref, w1_ref, w2_ref, gain_ref, shift_ref, cot_ref, mixed_ref,
    own, edge_l, edge_r, halo_l, halo_r, mid_l, mid_r, seam,
    digits, cots, acts, grads, w2p, w2t, back_w, ahead_w, p8, wt,
    gs, g_rs, g_z, g_ag, g_all,
    sg_send, sg_recv, af, af_send, af_recv, z_send, z_recv, ag,
    in_sem, out_sem, halo_send_sem, halo_recv_sem, send_sem, recv_sem,
):
    face, band = lax.axis_index("face"), lax.axis_index("band")
    core, z_hi, yx = face % 2, face // 2 % 2, face // 4
    y, x = yx // 4, yx % 4
    q, z = yx * 2 + core, z_hi * BANDS + band

    def plane(j):
        return (j // 2 * 4 + z_hi * 2 + j % 2, band)

    def line(j):
        return (yx * 4 + j // BANDS * 2 + core, j % BANDS)

    mates = [
        ((y + dy) % 4 * 4 + (x + dx) % 4) * 2 + (core + dc) % 2 for dy, dx, dc in PLANE_OFFSETS
    ]
    others = [(z + dz) % LINE for dz in LINE_OFFSETS]

    left, right = ((face + 63) % 64, band), ((face + 1) % 64, band)

    def half_way(seam_face):
        there = (seam_face // 2 % 2 * BANDS + band + 4) % LINE
        return (seam_face // 4 * 4 + there // BANDS * 2 + 1, there % BANDS)

    from_z = (z + 12) % LINE
    from_right = ((yx * 4 + from_z // BANDS * 2 + 2) % 64, from_z % BANDS)

    barrier = pltpu.get_barrier_semaphore()
    for target in (left, right):
        pl.semaphore_signal(barrier, 1, device_id=target, device_id_type=MESH)
    @pl.when(core == 1)
    def _():
        pl.semaphore_signal(barrier, 1, device_id=from_right, device_id_type=MESH)

    for j in others:
        pl.semaphore_signal(barrier, 1, device_id=line(j), device_id_type=MESH)
    for j in mates:
        pl.semaphore_signal(barrier, 1, device_id=plane(j), device_id_type=MESH)

    arrivals = [
        pltpu.make_async_copy(source, target, in_sem.at[k])
        for k, (source, target) in enumerate(
            [
                (code_in, code_ref), (proj_in, proj_ref), (w1_in, w1_ref), (w2_in, w2_ref),
                (gain_in, gain_ref), (shift_in, shift_ref), (cot_in, cot_ref),
            ]
        )
    ]
    for arrival in arrivals:
        arrival.start()

    def send(src, dst, sem, target):
        return pltpu.make_async_remote_copy(
            src, dst, send_sem.at[sem], recv_sem.at[sem], device_id=target, device_id_type=MESH
        )

    lane = iota((8, ROWS), 1)
    wide = iota((CH, ROWS), 1)

    arrivals[0].wait()
    codes = code_ref[0].astype(F32)
    own[...] = codes
    edge_l[...] = codes[0:2]
    edge_r[...] = codes[COLS - 2 : COLS]

    pl.semaphore_wait(barrier, PLANE - 1 + LINE - 1 + 2 + 1 - core)

    to_right = pltpu.make_async_remote_copy(
        edge_r, halo_l, halo_send_sem.at[0], halo_recv_sem.at[0], device_id=right, device_id_type=MESH
    )
    to_left = pltpu.make_async_remote_copy(
        edge_l, halo_r, halo_send_sem.at[1], halo_recv_sem.at[1], device_id=left, device_id_type=MESH
    )
    mid_right = pltpu.make_async_remote_copy(
        edge_r, mid_l, halo_send_sem.at[2], halo_recv_sem.at[2],
        device_id=half_way(face), device_id_type=MESH,
    )
    mid_left = pltpu.make_async_remote_copy(
        edge_l, mid_r, halo_send_sem.at[3], halo_recv_sem.at[3],
        device_id=half_way((face + 63) % 64), device_id_type=MESH,
    )

    @pl.when(core == 1)
    def _():
        mid_right.start()

    @pl.when(core == 0)
    def _():
        mid_left.start()

    to_left.start()
    to_right.start()

    for arrival in arrivals[1:]:
        arrival.wait()

    place, channel = iota((CH, CH), 0), iota((CH, CH), 1)
    perm = (channel == place % 32 // 4 * 12 + place // 32 * 4 + place % 4).astype(BF16)
    eye = (channel == place).astype(BF16)
    for dc in range(3):
        for dr in range(3):
            tap, at = dr * 3 + dc, dc * 3 + dr
            w2p[pl.ds(at * CH, CH), :] = dot(perm, w2_ref[tap]).astype(BF16)
            back = (2 - dc) * 3 + dr
            w2t[pl.ds(back * CH, CH), :] = dot_t(eye, w2p[pl.ds(at * CH, CH), :]).astype(BF16)
    ahead_w[...] = dot_t(eye, w2p[...]).astype(BF16)
    back_w[...] = dot_t(eye, w2t[...]).astype(BF16)

    level = jnp.where(iota((8, 1), 0) < 3, 8.0, 5.0)
    p8[...] = jnp.zeros_like(p8)
    p8[0:6, 0:CH] = proj_ref[...] / level[0:6]
    proj8 = p8[:, 0:CH]
    proj_parts = pieces(proj8, 3)
    proj_rows = jnp.concatenate(proj_parts + [jnp.zeros_like(proj8)], axis=0).astype(BF16)
    for dc in range(3):
        for dr in range(3):
            got = dot(proj_rows, w1_ref[dr * 3 + dc])
            wt[pl.ds(dc * 32 + dr * 8, 8), :] = got[0:8] + got[8:16] + got[16:24]
        wt[pl.ds(dc * 32 + 24, 8), :] = jnp.zeros((8, CH), F32)
    no_rows = jnp.zeros_like(proj8)
    lift_w = jnp.concatenate(
        [
            dot_t(eye, jnp.concatenate([no_rows, part, no_rows, no_rows], axis=0).astype(BF16))
            for part in proj_parts
        ],
        axis=0,
    ).astype(BF16)

    cots[0:2] = jnp.zeros((2, 3, CH, ROWS), BF16)
    cots[COLS + 2 : COLS + 4] = jnp.zeros((2, 3, CH, ROWS), BF16)

    def cot_step(c, carry):
        value = cot_ref[c]
        wider = value.astype(F32)
        cots[c + 2, 0] = earlier(wider, wide).astype(BF16)
        cots[c + 2, 1] = value
        cots[c + 2, 2] = later(wider, wide).astype(BF16)
        return carry

    lax.fori_loop(0, COLS, cot_step, 0)

    index = iota((8, 1), 0)
    stride = jnp.where(
        index == 0, 1.0, jnp.where(index == 1, 8.0, jnp.where(index == 2, 64.0,
        jnp.where(index == 3, 512.0, jnp.where(index == 4, 2560.0, 12800.0)))))
    per_stride, per_level = 1.0 / stride, 1.0 / level

    def decode(row):
        quotient = jnp.floor((row + 0.5) * per_stride)
        digit = quotient - level * jnp.floor((quotient + 0.5) * per_level)
        value = jnp.where(index < 6, 2.0 * digit - (level - 1.0), 0.0)
        block = [later(value, lane), jnp.where(index == 6, 1.0, value), earlier(value, lane)]
        return jnp.concatenate(block + [jnp.zeros_like(value)], axis=0).astype(BF16)

    for c in range(COLS):
        digits[c + 2] = decode(own[c : c + 1, :])

    @pl.when(core == 0)
    def _():
        to_left.wait_recv()
        seam[0:2, :] = own[COLS - 2 : COLS, :]
        seam[2:4, :] = halo_r[...]

    @pl.when(core == 1)
    def _():
        mid_right.wait_recv()
        mid_left.wait_recv()
        seam[0:2, :] = mid_l[...]
        seam[2:4, :] = mid_r[...]

    beside = [decode(seam[c : c + 1, :]) for c in range(4)]

    none = jnp.zeros((32, ROWS), BF16)

    def ahead(c):
        return jnp.concatenate(
            [digits[c + 2 + d] if c + d < COLS else none for d in range(3)] + [none], axis=0
        )

    gram = dot_t(
        jnp.concatenate([digits[c + 2] for c in range(COLS)] + beside[0:2], axis=1),
        jnp.concatenate(
            [ahead(c) for c in range(COLS)]
            + [
                jnp.concatenate([none, none, beside[2], none], axis=0),
                jnp.concatenate([none, beside[2], beside[3], none], axis=0),
            ],
            axis=1,
        ),
    )
    for j in range(PLANE):
        gs[j] = gram[j : j + 1]
    for j in mates:
        send(gs.at[j], g_rs.at[q], 0, plane(j)).start()
    g_rs[q] = gs[q]

    @pl.when(core == 1)
    def _():
        to_left.wait_recv()
        mid_right.wait_send()

    @pl.when(core == 0)
    def _():
        mid_left.wait_send()

    to_left.wait_send()
    to_right.wait()
    for c in range(2):
        digits[c] = decode(halo_l[c : c + 1, :])
        digits[COLS + 2 + c] = decode(halo_r[c : c + 1, :])

    def grad_step(step, carry):
        for k in range(6):
            c = step * 6 + k
            grads[c] = dot(back_w[...], cots[pl.ds(c, 3)].reshape(9 * CH, ROWS))
        return carry

    lax.fori_loop(0, 3, grad_step, 0)
    some = send(gs.at[pl.ds(0, PLANE - 1)], g_rs.at[pl.ds(0, PLANE - 1)], 0, right)
    some.wait()
    g_z[z] = jnp.sum(g_rs[...], axis=0)
    for j in others:
        send(g_z.at[z], g_z.at[z], 1, line(j)).start()
    send(g_z.at[pl.ds(0, LINE - 1)], g_z.at[pl.ds(0, LINE - 1)], 1, right).wait()
    g_ag[q] = jnp.sum(g_z[...], axis=0)
    for j in mates:
        send(g_ag.at[q], g_ag.at[q], 2, plane(j)).start()
    send(g_ag.at[pl.ds(0, PLANE - 1)], g_ag.at[pl.ds(0, PLANE - 1)], 2, right).wait()
    for j in range(PLANE):
        g_all[j : j + 1, :] = g_ag[j]
    g_all[PLANE:128, :] = jnp.zeros((128 - PLANE, 128), F32)

    near = g_all[0:32, :]
    flipped = jnp.transpose(g_all[...])
    lane32 = iota((32, 128), 1)
    gram_all = jnp.concatenate(
        [
            near,
            jnp.where(lane32 < 32, flipped[32:64], pltpu.roll(near, 32, 1)),
            jnp.where(
                lane32 < 32,
                flipped[64:96],
                jnp.where(lane32 < 64, pltpu.roll(flipped[32:64], 32, 1), pltpu.roll(near, 64, 1)),
            ),
        ],
        axis=0,
    )[:, 0:CH]
    digit_sum = gram_all[:, ONE : ONE + 1]
    digit_mean = digit_sum / POSITIONS
    covariance = gram_all / POSITIONS - digit_mean * (gram_all[ONE : ONE + 1, :] / POSITIONS)
    weights = wt[...]
    spread = dot32(covariance, weights)

    within = iota((8, 128), 1) % 3

    def by_group(value):
        row = jnp.concatenate([value, jnp.zeros((1, 128 - CH), F32)], axis=1)
        row = jnp.broadcast_to(row, (8, 128))
        next1, next2 = pltpu.roll(row, 127, 1), pltpu.roll(row, 126, 1)
        last1, last2 = pltpu.roll(row, 1, 1), pltpu.roll(row, 2, 1)
        first, middle, third = row + next1 + next2, last1 + row + next1, last2 + last1 + row
        return jnp.where(within == 0, first, jnp.where(within == 1, middle, third))[0:1, 0:CH]

    channel_mean = jnp.sum(weights * digit_mean, axis=0, keepdims=True)
    mean = by_group(channel_mean) / 3.0
    off = channel_mean - mean
    variance = by_group(jnp.sum(weights * spread, axis=0, keepdims=True) + off * off) / 3.0
    scale = 1.0 / jnp.sqrt(variance + 1e-05)
    gain = gain_ref[...]
    steep = scale * gain
    pre_w = jnp.where(place == ONE, shift_ref[...] - mean * steep, weights * steep)
    pre_w = jnp.concatenate(
        [dot_t(perm, part.astype(BF16)) for part in pieces(pre_w, 2)], axis=0
    ).astype(BF16)

    def act_step(step, total):
        for k in range(9):
            c = step * 9 + k
            taps = digits[pl.ds(c, 3)].reshape(CH, ROWS)
            both = dot(pre_w, taps)
            pre = both[0:CH] + both[CH : 2 * CH]
            sigma = 0.5 * jnp.tanh(0.5 * pre) + 0.5
            act = pre * sigma
            slope = sigma + act * (1.0 - sigma)
            acts[c, 0] = later(act, wide).astype(BF16)
            acts[c, 1] = act.astype(BF16)
            acts[c, 2] = earlier(act, wide).astype(BF16)
            total = total + dot_t(taps, (grads[c] * slope).astype(BF16))
        return total

    total = act_step(1, act_step(0, jnp.zeros((CH, CH), F32)))
    cot_all = jnp.concatenate([cot_ref[c] for c in range(COLS)], axis=1)
    sg_send[:, :, CH:128] = jnp.zeros((CHUNKS, 32, 128 - CH), BF16)
    for dc in range(3):
        if dc == 2:
            af[...] = jnp.zeros_like(af)
            af[0:CH, 0:CH] = dot32(total, perm.astype(F32))

            cot_sum = dot_t(jnp.concatenate([digits[c + 2] for c in range(COLS)], axis=1), cot_all)
            af[CH : CH + 8, 0:CH] = cot_sum[8:16]
            for j in range(PLANE - 1):
                af_send[j] = af[unit_row(j) : unit_row(j) + 2, :]
            af_send[PLANE - 1] = jnp.zeros((2, 128), F32)
            for j in mates:
                send(af_send.at[j], af_recv.at[q], 4, plane(j)).start()
        taps = [acts[c + dc].reshape(3 * CH, ROWS) for c in range(COLS)]
        got = dot_t(jnp.concatenate(taps, axis=1), cot_all)
        sg_send[9 * dc : 9 * dc + 9, :, 0:CH] = got.reshape(9, 32, CH).astype(BF16)
        for j in range(9 * dc, 9 * dc + 9):
            @pl.when(q != j)
            def _():
                send(sg_send.at[j], sg_recv.at[q], 3, plane(j)).start()
    af_recv[q] = af_send[q]

    @pl.when(q < CHUNKS)
    def _():
        sg_recv[q] = sg_send[q]

    def mixed_step(step, carry):
        for k in range(8):
            c = step * 8 + k
            out = dot(ahead_w[...], acts[pl.ds(c, 3)].reshape(9 * CH, ROWS))
            lift = dot(lift_w, digits[c + 2])
            lift = (lift[0:CH] + lift[CH : 2 * CH]) + lift[2 * CH : 3 * CH]
            mixed_ref[c] = (lift.astype(BF16).astype(F32) + out).astype(BF16)
        return carry

    lax.fori_loop(0, 2, mixed_step, 0)
    departure = pltpu.make_async_copy(mixed_ref, mixed_out, out_sem)
    departure.start()
    z_send[...] = jnp.zeros_like(z_send)

    @pl.when(q < CHUNKS)
    def _():
        send(sg_send.at[pl.ds(0, CHUNKS - 1)], sg_recv.at[pl.ds(0, CHUNKS - 1)], 3, right).wait_send()
        send(sg_recv.at[pl.ds(0, PLANE - 1)], sg_recv.at[pl.ds(0, PLANE - 1)], 3, right).wait_recv()

        def add(j, total):
            return total + sg_recv[j].astype(F32)

        total = lax.fori_loop(0, PLANE, add, jnp.zeros((32, 128), F32))
        for b in range(BANDS):
            z_send[b, 0:4] = total[4 * b : 4 * b + 4]

    @pl.when(q >= CHUNKS)
    def _():
        send(sg_send, sg_recv.at[pl.ds(0, CHUNKS)], 3, right).wait_send()

    send(af_send.at[pl.ds(0, PLANE - 1)], af_recv.at[pl.ds(0, PLANE - 1)], 4, right).wait()
    af_sum = jnp.sum(af_recv[...], axis=0)
    for b in range(BANDS):
        z_send[b, 4:6] = af_sum

    for j in others:
        send(z_send.at[j % BANDS], z_recv.at[z], 5, line(j)).start()
    z_recv[z] = z_send[band]
    send(z_recv.at[pl.ds(0, LINE - 1)], z_recv.at[pl.ds(0, LINE - 1)], 5, right).wait()
    ag[q] = jnp.sum(z_recv[...], axis=0)
    for j in mates:
        send(ag.at[q], ag.at[q], 6, plane(j)).start()
    standard_sum = scale * (POSITIONS * spread + digit_sum * off)
    chosen = iota((16, CH), 1) == band * 12 + iota((16, CH), 0)
    proj_band = dot32_t(chosen.astype(F32), proj8)
    send(ag.at[pl.ds(0, PLANE - 1)], ag.at[pl.ds(0, PLANE - 1)], 6, right).wait()

    for j in range(CHUNKS):
        tap = j // 3 % 3 * 3 + j // 9
        second_ref[tap, j % 3 * 4 : j % 3 * 4 + 4, :] = ag[j, 0:4, 0:CH]
    for j in range(PLANE - 1):
        af[unit_row(j) : unit_row(j) + 2, :] = ag[j, 4:6]

    sums = af[0:CH, 0:CH]
    shift_grad = af[ONE : ONE + 1, 0:CH]
    gain_grad = scale * (jnp.sum(weights * sums, axis=0, keepdims=True) - mean * shift_grad)
    shift_out[...] = shift_grad
    gain_out[...] = gain_grad
    count = 3.0 * POSITIONS
    first_mean = by_group(gain * shift_grad) / count
    second_mean = by_group(gain * gain_grad) / count
    grad_sum = scale * (gain * sums - first_mean * digit_sum - second_mean * standard_sum)

    back_sum = None
    for dc in range(3):
        for dr in range(3):
            part = grad_sum[dc * 32 + dr * 8 : dc * 32 + dr * 8 + 8]
            first_ref[dr * 3 + dc] = dot32(proj_band, part)[0:12]
            rows = jnp.concatenate(pieces(part, 3) + [no_rows], axis=0).astype(BF16)
            term = dot_t(rows, w1_ref[dr * 3 + dc])
            back_sum = term if back_sum is None else back_sum + term
    back_sum = back_sum[0:8] + back_sum[8:16] + back_sum[16:24] + af[CH : CH + 8, 0:CH]
    proj_out[...] = (back_sum / level)[0:6]
    departure.wait()


def write_out(*refs):
    sources, targets, held = refs[0:6], refs[6:12], refs[12:18]
    in_sem, out_sem = refs[18], refs[19]
    parts = [(k, None) for k in range(1, 6)] + [(0, pl.ds(2 * k, 2)) for k in range(8)]

    def view(group, part):
        which, rows = part
        return group[which] if rows is None else group[which].at[rows]

    ins = [
        pltpu.make_async_copy(view(sources, part), view(held, part), in_sem.at[k])
        for k, part in enumerate(parts)
    ]
    outs = [
        pltpu.make_async_copy(view(held, part), view(targets, part), out_sem.at[k])
        for k, part in enumerate(parts)
    ]
    for copy in ins:
        copy.start()
    for arrived, copy in zip(ins, outs):
        arrived.wait()
        copy.start()
    for copy in outs:
        copy.wait()


def body(code_ids, projection, first_weight, second_weight, norm_gain, norm_shift, cotangent):
    shape = jax.ShapeDtypeStruct
    vmem = pl.BlockSpec(memory_space=pltpu.VMEM)
    anywhere = pl.BlockSpec(memory_space=pltpu.HBM)
    operands = [
        jnp.swapaxes(code_ids, 1, 2),
        projection,
        first_weight,
        second_weight,
        norm_gain.reshape(1, CH),
        norm_shift.reshape(1, CH),
        cotangent,
    ]
    scratch = [pltpu.VMEM(operand.shape, operand.dtype) for operand in operands] + [
        pltpu.VMEM((COLS, CH, ROWS), BF16),
        pltpu.VMEM((COLS, ROWS), F32),
        pltpu.VMEM((2, ROWS), F32), pltpu.VMEM((2, ROWS), F32),
        pltpu.VMEM((2, ROWS), F32), pltpu.VMEM((2, ROWS), F32),
        pltpu.VMEM((2, ROWS), F32), pltpu.VMEM((2, ROWS), F32), pltpu.VMEM((4, ROWS), F32),
        pltpu.VMEM((COLS + 4, 32, ROWS), BF16),
        pltpu.VMEM((COLS + 4, 3, CH, ROWS), BF16),
        pltpu.VMEM((COLS + 2, 3, CH, ROWS), BF16),
        pltpu.VMEM((COLS + 2, CH, ROWS), F32),
        pltpu.VMEM((9 * CH, CH), BF16), pltpu.VMEM((9 * CH, CH), BF16),
        pltpu.VMEM((CH, 9 * CH), BF16), pltpu.VMEM((CH, 9 * CH), BF16),
        pltpu.VMEM((8, 128), F32), pltpu.VMEM((CH, CH), F32),
        pltpu.VMEM((PLANE, 1, 128), F32), pltpu.VMEM((PLANE, 1, 128), F32),
        pltpu.VMEM((LINE, 1, 128), F32), pltpu.VMEM((PLANE, 1, 128), F32),
        pltpu.VMEM((128, 128), F32),
        pltpu.VMEM((CHUNKS, 32, 128), BF16), pltpu.VMEM((PLANE, 32, 128), BF16),
        pltpu.VMEM((CH + 8, 128), F32),
        pltpu.VMEM((PLANE, 2, 128), F32), pltpu.VMEM((PLANE, 2, 128), F32),
        pltpu.VMEM((BANDS, 8, 128), F32), pltpu.VMEM((LINE, 8, 128), F32),
        pltpu.VMEM((PLANE, 8, 128), F32),
        pltpu.SemaphoreType.DMA((7,)), pltpu.SemaphoreType.DMA,
        pltpu.SemaphoreType.DMA((4,)), pltpu.SemaphoreType.DMA((4,)),
        pltpu.SemaphoreType.DMA((7,)), pltpu.SemaphoreType.DMA((7,)),
    ]
    outputs = [
        shape((COLS, CH, ROWS), BF16),
        shape((9, 12, CH), F32),
        shape((9, 12, CH), F32),
        shape((1, CH), F32),
        shape((1, CH), F32),
        shape((6, CH), F32),
    ]
    results = pl.pallas_call(
        kernel,
        out_shape=outputs,
        in_specs=[anywhere] * 7,
        out_specs=[anywhere] + [vmem] * 5,
        scratch_shapes=scratch,
        compiler_params=pltpu.CompilerParams(
            collective_id=0, has_side_effects=True, vmem_limit_bytes=VMEM_BYTES
        ),
        cost_estimate=pl.CostEstimate(
            flops=2_500_000_000, bytes_accessed=2_500_000, transcendentals=450_000
        ),
    )(*operands)
    mixed, first, second, gain_grad, shift_grad, proj = pl.pallas_call(
        write_out,
        out_shape=outputs,
        in_specs=[anywhere] * 6,
        out_specs=[anywhere] * 6,
        scratch_shapes=[pltpu.VMEM(output.shape, output.dtype) for output in outputs]
        + [pltpu.SemaphoreType.DMA((13,)), pltpu.SemaphoreType.DMA((13,))],
        compiler_params=pltpu.CompilerParams(vmem_limit_bytes=VMEM_BYTES),
    )(*results)
    return mixed, first, second, gain_grad.reshape(CH), shift_grad.reshape(CH), proj


def solution(mesh):
    return jax.shard_map(
        body,
        mesh=mesh,
        in_specs=(P("band", None, "face"), P(), P(), P(), P(), P(), P("face", "band", None)),
        out_specs=(
            P("face", "band", None),
            P(None, "band", None),
            P(None, "band", None),
            P(),
            P(),
            P(),
        ),
        check_vma=False,
    )
```

```python
import jax
import jax.numpy as jnp
from jax import lax
from jax.experimental import pallas as pl
from jax.experimental.pallas import tpu as pltpu
from jax.sharding import PartitionSpec as P

MESH = pl.DeviceIdType.MESH
HIGHEST = lax.Precision.HIGHEST
F32, BF16 = jnp.float32, jnp.bfloat16

CH, ROWS, COLS = 96, 256, 16
PLANE, LINE, BANDS = 32, 16, 8
CHUNKS = 27
POSITIONS = float(2**21)


def hops(step, ring):
    return min(step, ring - step)


PLANE_OFFSETS = sorted(
    [(dy, dx, dc) for dy in range(4) for dx in range(4) for dc in range(2) if dy + dx + dc > 0],
    key=lambda step: -4 * hops(step[0], 4) - 4 * hops(step[1], 4) - step[2],
)
LINE_OFFSETS = sorted(range(1, LINE), key=lambda step: -hops(step, LINE))
VMEM_BYTES = 64 * 1024 * 1024 - 65536
ONE = 46


def iota(shape, dim):
    return lax.broadcasted_iota(jnp.int32, shape, dim)


def dot(a, b):
    return lax.dot_general(a, b, (((1,), (0,)), ((), ())), preferred_element_type=F32)


def dot_t(a, b):
    return lax.dot_general(a, b, (((1,), (1,)), ((), ())), preferred_element_type=F32)


def dot32(a, b):
    return lax.dot_general(
        a, b, (((1,), (0,)), ((), ())), precision=HIGHEST, preferred_element_type=F32
    )


def dot32_t(a, b):
    return lax.dot_general(
        a, b, (((1,), (1,)), ((), ())), precision=HIGHEST, preferred_element_type=F32
    )


def pieces(value, count):
    parts = []
    for _ in range(count):
        part = value.astype(BF16).astype(F32)
        parts.append(part)
        value = value - part
    return parts


def later(value, lane):
    return jnp.where(lane == 0, 0.0, pltpu.roll(value, 1, 1))


def earlier(value, lane):
    return jnp.where(lane == ROWS - 1, 0.0, pltpu.roll(value, ROWS - 1, 1))


def unit_row(index):
    if index < 27:
        return index // 9 * 32 + index // 3 % 3 * 8 + index % 3 * 2
    return 96 + 2 * (index - 27) if index < 30 else ONE


def kernel(
    code_in, proj_in, w1_in, w2_in, gain_in, shift_in, cot_in,
    mixed_out, first_ref, second_ref, gain_out, shift_out, proj_out,
    code_ref, proj_ref, w1_ref, w2_ref, gain_ref, shift_ref, cot_ref, mixed_ref,
    own, edge_l, edge_r, halo_l, halo_r, mid_l, mid_r, seam,
    digits, cots, acts, grads, w2p, w2t, back_w, ahead_w, p8, wt,
    gs, g_rs, g_z, g_ag, g_all,
    sg_send, sg_recv, af, af_send, af_recv, z_send, z_recv, ag,
    in_sem, out_sem, halo_send_sem, halo_recv_sem, send_sem, recv_sem,
):
    face, band = lax.axis_index("face"), lax.axis_index("band")
    core, z_hi, yx = face % 2, face // 2 % 2, face // 4
    y, x = yx // 4, yx % 4
    q, z = yx * 2 + core, z_hi * BANDS + band

    def plane(j):
        return (j // 2 * 4 + z_hi * 2 + j % 2, band)

    def line(j):
        return (yx * 4 + j // BANDS * 2 + core, j % BANDS)

    mates = [
        ((y + dy) % 4 * 4 + (x + dx) % 4) * 2 + (core + dc) % 2 for dy, dx, dc in PLANE_OFFSETS
    ]
    others = [(z + dz) % LINE for dz in LINE_OFFSETS]

    left, right = ((face + 63) % 64, band), ((face + 1) % 64, band)

    def half_way(seam_face):
        there = (seam_face // 2 % 2 * BANDS + band + 4) % LINE
        return (seam_face // 4 * 4 + there // BANDS * 2 + 1, there % BANDS)

    from_z = (z + 12) % LINE
    from_right = ((yx * 4 + from_z // BANDS * 2 + 2) % 64, from_z % BANDS)

    barrier = pltpu.get_barrier_semaphore()
    for target in (left, right):
        pl.semaphore_signal(barrier, 1, device_id=target, device_id_type=MESH)
    @pl.when(core == 1)
    def _():
        pl.semaphore_signal(barrier, 1, device_id=from_right, device_id_type=MESH)

    for j in others:
        pl.semaphore_signal(barrier, 1, device_id=line(j), device_id_type=MESH)
    for j in mates:
        pl.semaphore_signal(barrier, 1, device_id=plane(j), device_id_type=MESH)

    arrivals = [
        pltpu.make_async_copy(source, target, in_sem.at[k])
        for k, (source, target) in enumerate(
            [
                (code_in, code_ref), (proj_in, proj_ref), (w1_in, w1_ref), (w2_in, w2_ref),
                (gain_in, gain_ref), (shift_in, shift_ref), (cot_in, cot_ref),
            ]
        )
    ]
    for arrival in arrivals:
        arrival.start()

    def send(src, dst, sem, target):
        return pltpu.make_async_remote_copy(
            src, dst, send_sem.at[sem], recv_sem.at[sem], device_id=target, device_id_type=MESH
        )

    lane = iota((8, ROWS), 1)
    wide = iota((CH, ROWS), 1)

    arrivals[0].wait()
    codes = code_ref[0].astype(F32)
    own[...] = codes
    edge_l[...] = codes[0:2]
    edge_r[...] = codes[COLS - 2 : COLS]

    pl.semaphore_wait(barrier, PLANE - 1 + LINE - 1 + 2 + 1 - core)

    to_right = pltpu.make_async_remote_copy(
        edge_r, halo_l, halo_send_sem.at[0], halo_recv_sem.at[0], device_id=right, device_id_type=MESH
    )
    to_left = pltpu.make_async_remote_copy(
        edge_l, halo_r, halo_send_sem.at[1], halo_recv_sem.at[1], device_id=left, device_id_type=MESH
    )
    mid_right = pltpu.make_async_remote_copy(
        edge_r, mid_l, halo_send_sem.at[2], halo_recv_sem.at[2],
        device_id=half_way(face), device_id_type=MESH,
    )
    mid_left = pltpu.make_async_remote_copy(
        edge_l, mid_r, halo_send_sem.at[3], halo_recv_sem.at[3],
        device_id=half_way((face + 63) % 64), device_id_type=MESH,
    )

    @pl.when(core == 1)
    def _():
        mid_right.start()

    @pl.when(core == 0)
    def _():
        mid_left.start()

    to_left.start()
    to_right.start()

    for arrival in arrivals[1:]:
        arrival.wait()

    place, channel = iota((CH, CH), 0), iota((CH, CH), 1)
    perm = (channel == place % 32 // 4 * 12 + place // 32 * 4 + place % 4).astype(BF16)
    eye = (channel == place).astype(BF16)
    for dc in range(3):
        for dr in range(3):
            tap, at = dr * 3 + dc, dc * 3 + dr
            w2p[pl.ds(at * CH, CH), :] = dot(perm, w2_ref[tap]).astype(BF16)
            back = (2 - dc) * 3 + dr
            w2t[pl.ds(back * CH, CH), :] = dot_t(eye, w2p[pl.ds(at * CH, CH), :]).astype(BF16)
    ahead_w[...] = dot_t(eye, w2p[...]).astype(BF16)
    back_w[...] = dot_t(eye, w2t[...]).astype(BF16)

    level = jnp.where(iota((8, 1), 0) < 3, 8.0, 5.0)
    p8[...] = jnp.zeros_like(p8)
    p8[0:6, 0:CH] = proj_ref[...] / level[0:6]
    proj8 = p8[:, 0:CH]
    proj_parts = pieces(proj8, 3)
    proj_rows = jnp.concatenate(proj_parts + [jnp.zeros_like(proj8)], axis=0).astype(BF16)
    for dc in range(3):
        for dr in range(3):
            got = dot(proj_rows, w1_ref[dr * 3 + dc])
            wt[pl.ds(dc * 32 + dr * 8, 8), :] = got[0:8] + got[8:16] + got[16:24]
        wt[pl.ds(dc * 32 + 24, 8), :] = jnp.zeros((8, CH), F32)
    no_rows = jnp.zeros_like(proj8)
    lift_w = jnp.concatenate(
        [
            dot_t(eye, jnp.concatenate([no_rows, part, no_rows, no_rows], axis=0).astype(BF16))
            for part in proj_parts
        ],
        axis=0,
    ).astype(BF16)

    cots[0:2] = jnp.zeros((2, 3, CH, ROWS), BF16)
    cots[COLS + 2 : COLS + 4] = jnp.zeros((2, 3, CH, ROWS), BF16)

    def cot_step(c, carry):
        value = cot_ref[c]
        wider = value.astype(F32)
        cots[c + 2, 0] = earlier(wider, wide).astype(BF16)
        cots[c + 2, 1] = value
        cots[c + 2, 2] = later(wider, wide).astype(BF16)
        return carry

    lax.fori_loop(0, COLS, cot_step, 0)

    index = iota((8, 1), 0)
    stride = jnp.where(
        index == 0, 1.0, jnp.where(index == 1, 8.0, jnp.where(index == 2, 64.0,
        jnp.where(index == 3, 512.0, jnp.where(index == 4, 2560.0, 12800.0)))))
    per_stride, per_level = 1.0 / stride, 1.0 / level

    def decode(row):
        quotient = jnp.floor((row + 0.5) * per_stride)
        digit = quotient - level * jnp.floor((quotient + 0.5) * per_level)
        value = jnp.where(index < 6, 2.0 * digit - (level - 1.0), 0.0)
        block = [later(value, lane), jnp.where(index == 6, 1.0, value), earlier(value, lane)]
        return jnp.concatenate(block + [jnp.zeros_like(value)], axis=0).astype(BF16)

    for c in range(COLS):
        digits[c + 2] = decode(own[c : c + 1, :])

    @pl.when(core == 0)
    def _():
        to_left.wait_recv()
        seam[0:2, :] = own[COLS - 2 : COLS, :]
        seam[2:4, :] = halo_r[...]

    @pl.when(core == 1)
    def _():
        mid_right.wait_recv()
        mid_left.wait_recv()
        seam[0:2, :] = mid_l[...]
        seam[2:4, :] = mid_r[...]

    beside = [decode(seam[c : c + 1, :]) for c in range(4)]

    none = jnp.zeros((32, ROWS), BF16)

    def ahead(c):
        return jnp.concatenate(
            [digits[c + 2 + d] if c + d < COLS else none for d in range(3)] + [none], axis=0
        )

    gram = dot_t(
        jnp.concatenate([digits[c + 2] for c in range(COLS)] + beside[0:2], axis=1),
        jnp.concatenate(
            [ahead(c) for c in range(COLS)]
            + [
                jnp.concatenate([none, none, beside[2], none], axis=0),
                jnp.concatenate([none, beside[2], beside[3], none], axis=0),
            ],
            axis=1,
        ),
    )
    for j in range(PLANE):
        gs[j] = gram[j : j + 1]
    for j in mates:
        send(gs.at[j], g_rs.at[q], 0, plane(j)).start()
    g_rs[q] = gs[q]

    @pl.when(core == 1)
    def _():
        to_left.wait_recv()
        mid_right.wait_send()

    @pl.when(core == 0)
    def _():
        mid_left.wait_send()

    to_left.wait_send()
    to_right.wait()
    for c in range(2):
        digits[c] = decode(halo_l[c : c + 1, :])
        digits[COLS + 2 + c] = decode(halo_r[c : c + 1, :])

    def grad_step(step, carry):
        for k in range(6):
            c = step * 6 + k
            grads[c] = dot(back_w[...], cots[pl.ds(c, 3)].reshape(9 * CH, ROWS))
        return carry

    lax.fori_loop(0, 3, grad_step, 0)
    some = send(gs.at[pl.ds(0, PLANE - 1)], g_rs.at[pl.ds(0, PLANE - 1)], 0, right)
    some.wait()
    g_z[z] = jnp.sum(g_rs[...], axis=0)
    for j in others:
        send(g_z.at[z], g_z.at[z], 1, line(j)).start()
    send(g_z.at[pl.ds(0, LINE - 1)], g_z.at[pl.ds(0, LINE - 1)], 1, right).wait()
    g_ag[q] = jnp.sum(g_z[...], axis=0)
    for j in mates:
        send(g_ag.at[q], g_ag.at[q], 2, plane(j)).start()
    send(g_ag.at[pl.ds(0, PLANE - 1)], g_ag.at[pl.ds(0, PLANE - 1)], 2, right).wait()
    for j in range(PLANE):
        g_all[j : j + 1, :] = g_ag[j]
    g_all[PLANE:128, :] = jnp.zeros((128 - PLANE, 128), F32)

    near = g_all[0:32, :]
    flipped = jnp.transpose(g_all[...])
    lane32 = iota((32, 128), 1)
    gram_all = jnp.concatenate(
        [
            near,
            jnp.where(lane32 < 32, flipped[32:64], pltpu.roll(near, 32, 1)),
            jnp.where(
                lane32 < 32,
                flipped[64:96],
                jnp.where(lane32 < 64, pltpu.roll(flipped[32:64], 32, 1), pltpu.roll(near, 64, 1)),
            ),
        ],
        axis=0,
    )[:, 0:CH]
    digit_sum = gram_all[:, ONE : ONE + 1]
    digit_mean = digit_sum / POSITIONS
    covariance = gram_all / POSITIONS - digit_mean * (gram_all[ONE : ONE + 1, :] / POSITIONS)
    weights = wt[...]
    spread = dot32(covariance, weights)

    within = iota((8, 128), 1) % 3

    def by_group(value):
        row = jnp.concatenate([value, jnp.zeros((1, 128 - CH), F32)], axis=1)
        row = jnp.broadcast_to(row, (8, 128))
        next1, next2 = pltpu.roll(row, 127, 1), pltpu.roll(row, 126, 1)
        last1, last2 = pltpu.roll(row, 1, 1), pltpu.roll(row, 2, 1)
        first, middle, third = row + next1 + next2, last1 + row + next1, last2 + last1 + row
        return jnp.where(within == 0, first, jnp.where(within == 1, middle, third))[0:1, 0:CH]

    channel_mean = jnp.sum(weights * digit_mean, axis=0, keepdims=True)
    mean = by_group(channel_mean) / 3.0
    off = channel_mean - mean
    variance = by_group(jnp.sum(weights * spread, axis=0, keepdims=True) + off * off) / 3.0
    scale = 1.0 / jnp.sqrt(variance + 1e-05)
    gain = gain_ref[...]
    steep = scale * gain
    pre_w = jnp.where(place == ONE, shift_ref[...] - mean * steep, weights * steep)
    pre_w = jnp.concatenate(
        [dot_t(perm, part.astype(BF16)) for part in pieces(pre_w, 2)], axis=0
    ).astype(BF16)

    def act_step(step, total):
        for k in range(9):
            c = step * 9 + k
            taps = digits[pl.ds(c, 3)].reshape(CH, ROWS)
            both = dot(pre_w, taps)
            pre = both[0:CH] + both[CH : 2 * CH]
            sigma = 0.5 * jnp.tanh(0.5 * pre) + 0.5
            act = pre * sigma
            slope = sigma + act * (1.0 - sigma)
            acts[c, 0] = later(act, wide).astype(BF16)
            acts[c, 1] = act.astype(BF16)
            acts[c, 2] = earlier(act, wide).astype(BF16)
            total = total + dot_t(taps, (grads[c] * slope).astype(BF16))
        return total

    total = act_step(1, act_step(0, jnp.zeros((CH, CH), F32)))
    cot_all = jnp.concatenate([cot_ref[c] for c in range(COLS)], axis=1)
    sg_send[:, :, CH:128] = jnp.zeros((CHUNKS, 32, 128 - CH), BF16)
    for dc in range(3):
        if dc == 2:
            af[...] = jnp.zeros_like(af)
            af[0:CH, 0:CH] = dot32(total, perm.astype(F32))

            cot_sum = dot_t(jnp.concatenate([digits[c + 2] for c in range(COLS)], axis=1), cot_all)
            af[CH : CH + 8, 0:CH] = cot_sum[8:16]
            for j in range(PLANE - 1):
                af_send[j] = af[unit_row(j) : unit_row(j) + 2, :]
            af_send[PLANE - 1] = jnp.zeros((2, 128), F32)
            for j in mates:
                send(af_send.at[j], af_recv.at[q], 4, plane(j)).start()
        taps = [acts[c + dc].reshape(3 * CH, ROWS) for c in range(COLS)]
        got = dot_t(jnp.concatenate(taps, axis=1), cot_all)
        sg_send[9 * dc : 9 * dc + 9, :, 0:CH] = got.reshape(9, 32, CH).astype(BF16)
        for k in range(9):
            j = 9 * dc + (q + k) % 9

            @pl.when(q != j)
            def _():
                send(sg_send.at[j], sg_recv.at[q], 3, plane(j)).start()
    af_recv[q] = af_send[q]

    @pl.when(q < CHUNKS)
    def _():
        sg_recv[q] = sg_send[q]

    def mixed_step(step, carry):
        for k in range(8):
            c = step * 8 + k
            out = dot(ahead_w[...], acts[pl.ds(c, 3)].reshape(9 * CH, ROWS))
            lift = dot(lift_w, digits[c + 2])
            lift = (lift[0:CH] + lift[CH : 2 * CH]) + lift[2 * CH : 3 * CH]
            mixed_ref[c] = (lift.astype(BF16).astype(F32) + out).astype(BF16)
        return carry

    lax.fori_loop(0, 2, mixed_step, 0)
    departure = pltpu.make_async_copy(mixed_ref, mixed_out, out_sem)
    departure.start()
    z_send[...] = jnp.zeros_like(z_send)

    @pl.when(q < CHUNKS)
    def _():
        send(sg_send.at[pl.ds(0, CHUNKS - 1)], sg_recv.at[pl.ds(0, CHUNKS - 1)], 3, right).wait_send()
        send(sg_recv.at[pl.ds(0, PLANE - 1)], sg_recv.at[pl.ds(0, PLANE - 1)], 3, right).wait_recv()

        def add(j, total):
            return total + sg_recv[j].astype(F32)

        total = lax.fori_loop(0, PLANE, add, jnp.zeros((32, 128), F32))
        for b in range(BANDS):
            z_send[b, 0:4] = total[4 * b : 4 * b + 4]

    @pl.when(q >= CHUNKS)
    def _():
        send(sg_send, sg_recv.at[pl.ds(0, CHUNKS)], 3, right).wait_send()

    send(af_send.at[pl.ds(0, PLANE - 1)], af_recv.at[pl.ds(0, PLANE - 1)], 4, right).wait()
    af_sum = jnp.sum(af_recv[...], axis=0)
    for b in range(BANDS):
        z_send[b, 4:6] = af_sum

    for j in others:
        send(z_send.at[j % BANDS], z_recv.at[z], 5, line(j)).start()
    z_recv[z] = z_send[band]
    send(z_recv.at[pl.ds(0, LINE - 1)], z_recv.at[pl.ds(0, LINE - 1)], 5, right).wait()
    ag[q] = jnp.sum(z_recv[...], axis=0)
    for j in mates:
        send(ag.at[q], ag.at[q], 6, plane(j)).start()
    standard_sum = scale * (POSITIONS * spread + digit_sum * off)
    chosen = iota((16, CH), 1) == band * 12 + iota((16, CH), 0)
    proj_band = dot32_t(chosen.astype(F32), proj8)
    send(ag.at[pl.ds(0, PLANE - 1)], ag.at[pl.ds(0, PLANE - 1)], 6, right).wait()

    for j in range(CHUNKS):
        tap = j // 3 % 3 * 3 + j // 9
        second_ref[tap, j % 3 * 4 : j % 3 * 4 + 4, :] = ag[j, 0:4, 0:CH]
    for j in range(PLANE - 1):
        af[unit_row(j) : unit_row(j) + 2, :] = ag[j, 4:6]

    sums = af[0:CH, 0:CH]
    shift_grad = af[ONE : ONE + 1, 0:CH]
    gain_grad = scale * (jnp.sum(weights * sums, axis=0, keepdims=True) - mean * shift_grad)
    shift_out[...] = shift_grad
    gain_out[...] = gain_grad
    count = 3.0 * POSITIONS
    first_mean = by_group(gain * shift_grad) / count
    second_mean = by_group(gain * gain_grad) / count
    grad_sum = scale * (gain * sums - first_mean * digit_sum - second_mean * standard_sum)

    back_sum = None
    for dc in range(3):
        for dr in range(3):
            part = grad_sum[dc * 32 + dr * 8 : dc * 32 + dr * 8 + 8]
            first_ref[dr * 3 + dc] = dot32(proj_band, part)[0:12]
            rows = jnp.concatenate(pieces(part, 3) + [no_rows], axis=0).astype(BF16)
            term = dot_t(rows, w1_ref[dr * 3 + dc])
            back_sum = term if back_sum is None else back_sum + term
    back_sum = back_sum[0:8] + back_sum[8:16] + back_sum[16:24] + af[CH : CH + 8, 0:CH]
    proj_out[...] = (back_sum / level)[0:6]
    departure.wait()


def write_out(*refs):
    sources, targets, held = refs[0:6], refs[6:12], refs[12:18]
    in_sem, out_sem = refs[18], refs[19]
    parts = [(k, None) for k in range(1, 6)] + [(0, pl.ds(2 * k, 2)) for k in range(8)]

    def view(group, part):
        which, rows = part
        return group[which] if rows is None else group[which].at[rows]

    ins = [
        pltpu.make_async_copy(view(sources, part), view(held, part), in_sem.at[k])
        for k, part in enumerate(parts)
    ]
    outs = [
        pltpu.make_async_copy(view(held, part), view(targets, part), out_sem.at[k])
        for k, part in enumerate(parts)
    ]
    for copy in ins:
        copy.start()
    for arrived, copy in zip(ins, outs):
        arrived.wait()
        copy.start()
    for copy in outs:
        copy.wait()


def body(code_ids, projection, first_weight, second_weight, norm_gain, norm_shift, cotangent):
    shape = jax.ShapeDtypeStruct
    vmem = pl.BlockSpec(memory_space=pltpu.VMEM)
    anywhere = pl.BlockSpec(memory_space=pltpu.HBM)
    operands = [
        jnp.swapaxes(code_ids, 1, 2),
        projection,
        first_weight,
        second_weight,
        norm_gain.reshape(1, CH),
        norm_shift.reshape(1, CH),
        cotangent,
    ]
    scratch = [pltpu.VMEM(operand.shape, operand.dtype) for operand in operands] + [
        pltpu.VMEM((COLS, CH, ROWS), BF16),
        pltpu.VMEM((COLS, ROWS), F32),
        pltpu.VMEM((2, ROWS), F32), pltpu.VMEM((2, ROWS), F32),
        pltpu.VMEM((2, ROWS), F32), pltpu.VMEM((2, ROWS), F32),
        pltpu.VMEM((2, ROWS), F32), pltpu.VMEM((2, ROWS), F32), pltpu.VMEM((4, ROWS), F32),
        pltpu.VMEM((COLS + 4, 32, ROWS), BF16),
        pltpu.VMEM((COLS + 4, 3, CH, ROWS), BF16),
        pltpu.VMEM((COLS + 2, 3, CH, ROWS), BF16),
        pltpu.VMEM((COLS + 2, CH, ROWS), F32),
        pltpu.VMEM((9 * CH, CH), BF16), pltpu.VMEM((9 * CH, CH), BF16),
        pltpu.VMEM((CH, 9 * CH), BF16), pltpu.VMEM((CH, 9 * CH), BF16),
        pltpu.VMEM((8, 128), F32), pltpu.VMEM((CH, CH), F32),
        pltpu.VMEM((PLANE, 1, 128), F32), pltpu.VMEM((PLANE, 1, 128), F32),
        pltpu.VMEM((LINE, 1, 128), F32), pltpu.VMEM((PLANE, 1, 128), F32),
        pltpu.VMEM((128, 128), F32),
        pltpu.VMEM((CHUNKS, 32, 128), BF16), pltpu.VMEM((PLANE, 32, 128), BF16),
        pltpu.VMEM((CH + 8, 128), F32),
        pltpu.VMEM((PLANE, 2, 128), F32), pltpu.VMEM((PLANE, 2, 128), F32),
        pltpu.VMEM((BANDS, 8, 128), F32), pltpu.VMEM((LINE, 8, 128), F32),
        pltpu.VMEM((PLANE, 8, 128), F32),
        pltpu.SemaphoreType.DMA((7,)), pltpu.SemaphoreType.DMA,
        pltpu.SemaphoreType.DMA((4,)), pltpu.SemaphoreType.DMA((4,)),
        pltpu.SemaphoreType.DMA((7,)), pltpu.SemaphoreType.DMA((7,)),
    ]
    outputs = [
        shape((COLS, CH, ROWS), BF16),
        shape((9, 12, CH), F32),
        shape((9, 12, CH), F32),
        shape((1, CH), F32),
        shape((1, CH), F32),
        shape((6, CH), F32),
    ]
    results = pl.pallas_call(
        kernel,
        out_shape=outputs,
        in_specs=[anywhere] * 7,
        out_specs=[anywhere] + [vmem] * 5,
        scratch_shapes=scratch,
        compiler_params=pltpu.CompilerParams(
            collective_id=0, has_side_effects=True, vmem_limit_bytes=VMEM_BYTES
        ),
        cost_estimate=pl.CostEstimate(
            flops=2_500_000_000, bytes_accessed=2_500_000, transcendentals=450_000
        ),
    )(*operands)
    mixed, first, second, gain_grad, shift_grad, proj = pl.pallas_call(
        write_out,
        out_shape=outputs,
        in_specs=[anywhere] * 6,
        out_specs=[anywhere] * 6,
        scratch_shapes=[pltpu.VMEM(output.shape, output.dtype) for output in outputs]
        + [pltpu.SemaphoreType.DMA((13,)), pltpu.SemaphoreType.DMA((13,))],
        compiler_params=pltpu.CompilerParams(vmem_limit_bytes=VMEM_BYTES),
    )(*results)
    return mixed, first, second, gain_grad.reshape(CH), shift_grad.reshape(CH), proj


def solution(mesh):
    return jax.shard_map(
        body,
        mesh=mesh,
        in_specs=(P("band", None, "face"), P(), P(), P(), P(), P(), P("face", "band", None)),
        out_specs=(
            P("face", "band", None),
            P(None, "band", None),
            P(None, "band", None),
            P(),
            P(),
            P(),
        ),
        check_vma=False,
    )
```
